128 devices in a mesh: dp: 4 (over x_hi, core), head: 4 (over y), ctx: 8 (over x_lo, z).
Axes of the slice: x: 4 (x_hi: 2, x_lo: 2; x = x_hi * 2 + x_lo), y: 4, z: 4, core: 2. Of those that a mesh axis runs over, the one named last changes fastest.
Arguments:
- hidden_in: bfloat16 [4, 2048, 12288], P('dp', 'ctx'), may hold values from -6 to 6
- queries: bfloat16 [4, 2048, 6144], P('dp', 'ctx', 'head')
- rotary_key_rows: bfloat16 [4, 2048, 512], P('dp', 'ctx', 'head'), may hold values from -4.5 to 4.5
- value_projection: bfloat16 [12288, 512], P(('dp', 'ctx'), 'head'), may hold values from -0.0546875 to 0.0546875
- output_gradient: bfloat16 [4, 2048, 6144], P('dp', 'ctx', 'head'), may hold values from -1.5 to 1.5
- attended: bfloat16 [4, 2048, 6144], P('dp', 'ctx', 'head'), may hold values from -6 to 6
- doc_ids: int32 [4, 2048], P('dp'), may hold values from 0 to 5, never falling along the last dimension, each value on 1 to 1024 neighbouring positions
- block_place: int32 [4, 16], P('dp'), may hold values from 0 to 15, each once within a row
Outputs:
- query_gradient_rows: bfloat16 [4, 2048, 6144], P('dp', 'ctx', 'head')
- key_gradient_rows: bfloat16 [4, 2048, 512], P('dp', 'ctx', 'head')
- input_grad: bfloat16 [4, 2048, 12288], P('dp', 'ctx', 'head')
- weight_grad: float32 [12288, 512], P(('dp', 'ctx'), 'head')
The draws below stay inside these ranges and needn't reach their ends.
Inputs may be any that keep to these rules, and one draw needn't show every extreme that they name: `doc_ids`: along each sequence the document numbers never fall; no document holds more than 1024 positions and one holds exactly that many. `block_place`: each row names every place 0 to 15 once.
All inputs are finite; a program needn't handle non-finite values.
Results may differ from the reference program's by a relative error of at most 0.02.
Values may be sent and summed in bfloat16 or wider, within the bound.
No kernel may reach another device: no remote copies, remote signals or barrier semaphores. Data moves between devices by JAX's collectives and lax.ppermute only.
A program may use at most 128 MiB of HBM per device.

```python
import math
import jax
import jax.numpy as jnp
import numpy as np
from jax import lax

MODEL_WIDTH = 12288
HEAD_SIZE = 128
QUERY_PER_KEY = 12
KEY_VALUE_HEADS = 4
QUERY_HEADS = 48
SEQUENCE_LENGTH = 2048
BLOCK_ROWS = 128
BLOCKS = 16
SEQUENCE_COUNT = 4
DOCS = 6


def key_base(key):
    random_base = jax.random.normal(jax.random.fold_in(key, 11), (SEQUENCE_COUNT, SEQUENCE_LENGTH, KEY_VALUE_HEADS * HEAD_SIZE), jnp.float32)
    return jnp.clip(random_base, -4.5, 4.5)


def draw_rotary_key_rows(key, part):
    random_base = key_base(key)
    return random_base.astype(jnp.bfloat16)


def draw_queries(key, part):
    key = jax.random.fold_in(key, 2)
    sample = jnp.clip(jax.random.normal(key, (SEQUENCE_COUNT, SEQUENCE_LENGTH, QUERY_HEADS * HEAD_SIZE), jnp.float32), -4.5, 4.5)
    return sample.astype(jnp.bfloat16)


def spiked(entries, own_key, source, target, blocks, factor):
    def block_of(axis_at):
        return (jnp.arange(entries.shape[axis_at]) // (entries.shape[axis_at] // blocks)).reshape((-1,) + (1,) * (entries.ndim - 1 - axis_at))

    one_side = jax.random.permutation(own_key, blocks)[block_of(target)]
    second = (block_of(target) + blocks // 2) % blocks
    return jnp.where((block_of(source) == one_side) | (block_of(source) == second), factor * entries, entries)


def shard_levels(own_key, shape, shards, low, largest):
    def one(position, shards_of):
        draws = jax.random.uniform(jax.random.fold_in(jax.random.fold_in(own_key, 6), position), (shards_of,), jnp.float32, low / len(shards), largest / len(shards))
        return jnp.repeat(jnp.exp(draws), shape[position] // shards_of).reshape((-1,) + (1,) * (len(shape) - position - 1))

    factor_of = one(*shards[0])
    for cut in shards[1:]:
        factor_of = factor_of * one(*cut)
    return factor_of


def split_up(number_of, total, reach, skew):
    loads = [(1 << 20) // math.isqrt(rank ** skew) + 1 for rank in range(2, number_of + 1)]
    spare, given = total - reach - (number_of - 1), [1] * (number_of - 1)
    while spare > 0:
        movable = [i for i in range(number_of - 1) if given[i] < reach]
        pool, budget = sum([loads[i] for i in movable]), spare
        for i in movable:
            extra = min(reach - given[i], max(1, budget * loads[i] // pool), spare)
            given[i] = given[i] + extra
            spare = spare - extra
    return np.array([reach] + given)


def uneven(rng, amount, total, limit, skew):
    if amount == 2:
        one = jax.random.randint(rng, (), max(1, total - limit), min(limit, total - 1) + 1)
        return jnp.stack([one, total - one])
    lengths = jnp.asarray(split_up(amount, total, limit, skew), jnp.int32)
    couples = (amount - 1) // 2
    giver, taker = lengths[1:1 + 2 * couples:2], lengths[2:2 + 2 * couples:2]
    margin = jnp.minimum(giver - 1, limit - taker)
    moved = jax.random.randint(jax.random.fold_in(rng, 1), (couples,), 0, 1 << 20) % (margin + 1)
    lengths = lengths.at[1:1 + 2 * couples:2].set(giver - moved).at[2:2 + 2 * couples:2].set(taker + moved)
    return lengths[jax.random.permutation(jax.random.fold_in(rng, 2), amount)]


def centred(own_key, extent, scale, reach, cuts=(), kind=jnp.bfloat16):
    gain = shard_levels(own_key, extent, cuts, -0.22, 0.18) if cuts else 1.0
    values = jax.random.normal(own_key, extent, jnp.float32) * scale * gain
    return jnp.minimum(jnp.maximum(values, -reach), reach).astype(kind)


def gaussian_with(key, extent, deviation, reach, cuts, heavy, kind=jnp.bfloat16):
    array = deviation * jax.random.normal(key, extent, jnp.float32)
    if cuts:
        array = array * shard_levels(key, extent, cuts, -0.22, 0.18)
    return jnp.clip(spiked(array, jax.random.fold_in(key, 3), *heavy), -reach, reach).astype(kind)


def setup_inputs(seed: int = 0) -> dict:
    arg_keys = jax.random.split(jax.random.key(seed), 9)
    hidden_in = gaussian_with(arg_keys[0], (SEQUENCE_COUNT, SEQUENCE_LENGTH, MODEL_WIDTH), 1.0, 6.0, ((0, 4), (1, 8)), (1, 2, 8, 2.0))
    queries = draw_queries(jax.random.fold_in(arg_keys[8], 71), 0)
    rotary_key_rows = draw_rotary_key_rows(jax.random.fold_in(arg_keys[8], 71), 0)
    value_projection = centred(arg_keys[3], (MODEL_WIDTH, KEY_VALUE_HEADS * HEAD_SIZE), MODEL_WIDTH ** -0.5, 0.0546875, ((0, 32), (1, 4)))
    output_gradient = centred(arg_keys[4], (SEQUENCE_COUNT, SEQUENCE_LENGTH, QUERY_HEADS * HEAD_SIZE), 0.25, 1.5, ((0, 4), (1, 8), (2, 4)))
    attended = centred(arg_keys[5], (SEQUENCE_COUNT, SEQUENCE_LENGTH, QUERY_HEADS * HEAD_SIZE), 1.0, 6.0, ((0, 4), (1, 8), (2, 4)))
    doc_ids = jax.vmap(lambda own: jnp.searchsorted(jnp.cumsum(uneven(own, DOCS, SEQUENCE_LENGTH, SEQUENCE_LENGTH // 2, 1)), jnp.arange(SEQUENCE_LENGTH), side="right"))(jax.random.split(arg_keys[6], SEQUENCE_COUNT)).reshape((SEQUENCE_COUNT, SEQUENCE_LENGTH)).astype(jnp.int32)
    block_place = jax.vmap(lambda own: jax.random.permutation(own, BLOCKS))(jax.random.split(arg_keys[7], SEQUENCE_COUNT)).reshape((SEQUENCE_COUNT, BLOCKS)).astype(jnp.int32)
    return {"hidden_in": hidden_in, "queries": queries, "rotary_key_rows": rotary_key_rows, "value_projection": value_projection, "output_gradient": output_gradient, "attended": attended, "doc_ids": doc_ids, "block_place": block_place}


def attend(packed):
    query_block, key_block, value_block, grad_block, saved_block, position_index, document_labels = packed
    scaling = float(HEAD_SIZE) ** -0.5
    visible = (position_index[None, :] <= position_index[:, None]) & (document_labels[None, :] == document_labels[:, None])
    query_full = query_block.astype(jnp.float32)
    key_full = key_block.astype(jnp.float32)
    value_full = value_block.astype(jnp.float32)
    grad_full = grad_block.astype(jnp.float32)
    logits = jnp.einsum("gqd,kd->gqk", query_full, key_full) * scaling
    log_total = jax.nn.logsumexp(jnp.where(visible, logits, -jnp.inf), axis=-1)
    probs = jnp.where(visible, jnp.exp(logits - log_total[..., None]), 0.0)
    prob_half = probs.astype(jnp.bfloat16)
    row_terms = jnp.sum(grad_full * saved_block.astype(jnp.float32), axis=-1)
    dprobs = jnp.einsum("gqd,kd->gqk", grad_full, value_full)
    dscores = (probs * (dprobs - row_terms[..., None])).astype(jnp.bfloat16).astype(jnp.float32)
    query_gradient = (jnp.einsum("gqk,kd->gqd", dscores, key_full) * scaling).astype(jnp.bfloat16)
    key_gradient = (jnp.einsum("gqk,gqd->kd", dscores, query_full) * scaling).astype(jnp.bfloat16)
    value_gradient = jnp.einsum("gqk,gqd->kd", prob_half.astype(jnp.float32), grad_full).astype(jnp.bfloat16)
    return query_gradient, key_gradient, value_gradient


def reference(hidden_in, queries, rotary_key_rows, value_projection, output_gradient, attended, doc_ids, block_place):
    flat_inputs = hidden_in.reshape(SEQUENCE_COUNT * SEQUENCE_LENGTH, MODEL_WIDTH)
    value_matrix = jnp.dot(flat_inputs, value_projection, preferred_element_type=jnp.float32).astype(jnp.bfloat16)
    value_matrix = value_matrix.reshape(SEQUENCE_COUNT, SEQUENCE_LENGTH, KEY_VALUE_HEADS * HEAD_SIZE)
    row_index = jnp.arange(SEQUENCE_LENGTH, dtype=jnp.int32)
    position_index = (block_place[:, row_index // BLOCK_ROWS] * BLOCK_ROWS + row_index % BLOCK_ROWS).astype(jnp.int32)
    document_labels = jnp.take_along_axis(doc_ids, position_index, axis=1)
    query_batch = queries.reshape(SEQUENCE_COUNT, SEQUENCE_LENGTH, KEY_VALUE_HEADS, QUERY_PER_KEY, HEAD_SIZE).transpose(0, 2, 3, 1, 4).reshape(SEQUENCE_COUNT * KEY_VALUE_HEADS, QUERY_PER_KEY, SEQUENCE_LENGTH, HEAD_SIZE)
    gradient_batch = output_gradient.reshape(SEQUENCE_COUNT, SEQUENCE_LENGTH, KEY_VALUE_HEADS, QUERY_PER_KEY, HEAD_SIZE).transpose(0, 2, 3, 1, 4).reshape(SEQUENCE_COUNT * KEY_VALUE_HEADS, QUERY_PER_KEY, SEQUENCE_LENGTH, HEAD_SIZE)
    saved_batch = attended.reshape(SEQUENCE_COUNT, SEQUENCE_LENGTH, KEY_VALUE_HEADS, QUERY_PER_KEY, HEAD_SIZE).transpose(0, 2, 3, 1, 4).reshape(SEQUENCE_COUNT * KEY_VALUE_HEADS, QUERY_PER_KEY, SEQUENCE_LENGTH, HEAD_SIZE)
    key_batch = rotary_key_rows.reshape(SEQUENCE_COUNT, SEQUENCE_LENGTH, KEY_VALUE_HEADS, HEAD_SIZE).transpose(0, 2, 1, 3).reshape(SEQUENCE_COUNT * KEY_VALUE_HEADS, SEQUENCE_LENGTH, HEAD_SIZE)
    value_batch = value_matrix.reshape(SEQUENCE_COUNT, SEQUENCE_LENGTH, KEY_VALUE_HEADS, HEAD_SIZE).transpose(0, 2, 1, 3).reshape(SEQUENCE_COUNT * KEY_VALUE_HEADS, SEQUENCE_LENGTH, HEAD_SIZE)
    position_batch = jnp.repeat(position_index, KEY_VALUE_HEADS, axis=0)
    document_batch = jnp.repeat(document_labels, KEY_VALUE_HEADS, axis=0)
    query_gradient, key_gradient, value_gradient = lax.map(attend, (query_batch, key_batch, value_batch, gradient_batch, saved_batch, position_batch, document_batch))
    query_gradient_rows = query_gradient.reshape(SEQUENCE_COUNT, KEY_VALUE_HEADS, QUERY_PER_KEY, SEQUENCE_LENGTH, HEAD_SIZE).transpose(0, 3, 1, 2, 4).reshape(SEQUENCE_COUNT, SEQUENCE_LENGTH, QUERY_HEADS * HEAD_SIZE)
    key_gradient_rows = key_gradient.reshape(SEQUENCE_COUNT, KEY_VALUE_HEADS, SEQUENCE_LENGTH, HEAD_SIZE).transpose(0, 2, 1, 3).reshape(SEQUENCE_COUNT, SEQUENCE_LENGTH, KEY_VALUE_HEADS * HEAD_SIZE)
    value_gradient_rows = value_gradient.reshape(SEQUENCE_COUNT, KEY_VALUE_HEADS, SEQUENCE_LENGTH, HEAD_SIZE).transpose(0, 2, 1, 3).reshape(SEQUENCE_COUNT * SEQUENCE_LENGTH, KEY_VALUE_HEADS * HEAD_SIZE)
    grad_scale = float(SEQUENCE_COUNT * SEQUENCE_LENGTH) ** -0.5
    weight_grad = jnp.dot(flat_inputs.T, value_gradient_rows, preferred_element_type=jnp.float32) * grad_scale
    input_grad = jnp.dot(value_gradient_rows, value_projection.T, preferred_element_type=jnp.float32).astype(jnp.bfloat16)
    return query_gradient_rows, key_gradient_rows, input_grad.reshape(SEQUENCE_COUNT, SEQUENCE_LENGTH, MODEL_WIDTH), weight_grad
```

```python
import jax
import jax.numpy as jnp
from jax import lax
from jax.experimental import pallas as pl
from jax.experimental.pallas import tpu as pltpu
from jax.sharding import PartitionSpec as P

HEAD_SIZE = 128
QUERY_PER_KEY = 12
PAIRS = QUERY_PER_KEY // 2
BLOCK = 128
WINDOW = 9
SPAN = WINDOW * BLOCK
SLAB = 384
MASKED = -1e30
LOG2E = 1.4426950408889634
SCALING = float(HEAD_SIZE) ** (-0.5)
f32 = jnp.float32
bf16 = jnp.bfloat16


def place_of(index):
    dp, ctx = divmod(index, 8)
    x_hi, core = divmod(dp, 2)
    x_lo, z = divmod(ctx, 4)
    return x_hi * 2 + x_lo, z, core


def index_of(x, z, core):
    x_hi, x_lo = divmod(x % 4, 2)
    return (x_hi * 2 + core) * 8 + x_lo * 4 + z % 4


def moved(value, where):
    pairs = [(i, index_of(*where(*place_of(i)))) for i in range(32)]
    return lax.ppermute(value, ("dp", "ctx"), pairs)


def core_swap(value):
    return moved(value, lambda x, z, c: (x, z, 1 - c))


def x_swap(value):
    return moved(value, lambda x, z, c: (x ^ 1, z, c))


def z_step(value, by):
    return moved(value, lambda x, z, c: (x, z + by, c))


def first_step(value, by):
    return moved(value, lambda x, z, c: (x, z + by, c) if c == 0 else (x + by, z, c))


def second_step(value, by):
    return moved(value, lambda x, z, c: (x + by, z, c) if c == 0 else (x, z + by, c))


def nt(a, b):
    return lax.dot_general(a, b, (((1,), (1,)), ((), ())), preferred_element_type=f32)


def nn(a, b):
    return lax.dot_general(a, b, (((1,), (0,)), ((), ())), preferred_element_type=f32)


def tn(a, b):
    return lax.dot_general(a, b, (((0,), (0,)), ((), ())), preferred_element_type=f32)


def row_terms_kernel(grad_ref, saved_ref, out_ref):
    for a in range(2):
        for pair in range(PAIRS):
            for half in range(2):
                rows = slice(a * BLOCK, (a + 1) * BLOCK)
                cols = slice((2 * pair + half) * HEAD_SIZE, (2 * pair + half + 1) * HEAD_SIZE)
                product = grad_ref[rows, cols].astype(f32) * saved_ref[rows, cols].astype(f32)
                out_ref[a * PAIRS + pair : a * PAIRS + pair + 1, half * BLOCK : (half + 1) * BLOCK] = (
                    jnp.sum(product.T, axis=0, keepdims=True)
                )


def fill_bias(place, doc_ref, bias_ref):
    docs = doc_ref[...]
    own = doc_ref[pl.ds(place, 1), :]
    start = jnp.zeros((1, BLOCK), f32)
    for d in range(1, 6):
        held = jnp.sum(jnp.where(docs == d - 1, 1.0, 0.0), axis=(0, 1), keepdims=True)
        start = start + jnp.where(own >= d, held, 0.0)
    start = start.astype(jnp.int32)
    query = place * BLOCK + lax.broadcasted_iota(jnp.int32, (1, BLOCK), 1)
    key = (place - (WINDOW - 1)) * BLOCK + lax.broadcasted_iota(jnp.int32, (SPAN, 1), 0)
    bias_ref[...] = jnp.where((key >= start) & (key <= query), 0.0, MASKED)


def fill_window(table_ref, place, parts, win_ref):
    for j in range(WINDOW):
        block = table_ref[jnp.maximum(place - (WINDOW - 1) + j, 0)]
        win_ref[j * BLOCK : (j + 1) * BLOCK, :] = parts[pl.ds(pl.multiple_of(block * BLOCK, BLOCK), BLOCK), :]


def join(parts, all_ref):
    rows = parts[0].shape[0]
    for i, part in enumerate(parts):
        all_ref[i * rows : (i + 1) * rows, :] = part[...]


def head_pair(ref, a, pair):
    rows = slice(a * BLOCK, (a + 1) * BLOCK)
    one = ref[rows, pl.ds(pl.multiple_of(pair * 256, 256), HEAD_SIZE)]
    two = ref[rows, pl.ds(pl.multiple_of(pair * 256 + 128, 128), HEAD_SIZE)]
    return jnp.concatenate([one, two], axis=0)


def add_window(table_ref, place, win_ref, sum_ref):
    for j in range(WINDOW):
        block = table_ref[jnp.maximum(place - (WINDOW - 1) + j, 0)]
        at = pl.ds(pl.multiple_of(block * BLOCK, BLOCK), BLOCK)
        sum_ref[at, :] += win_ref[j * BLOCK : (j + 1) * BLOCK, :]


def value_side_kernel(
    table_ref, doc_ref, q_ref, g_ref, k0, k1, k2, k3,
    total_ref, o0, o1, o2, o3, all_ref, win_ref, bias_ref, acc_ref, sum_ref,
):
    join((k0, k1, k2, k3), all_ref)
    sum_ref[...] = jnp.zeros_like(sum_ref)
    for a in range(2):
        place = table_ref[16 + a]
        fill_bias(place, doc_ref, bias_ref)
        fill_window(table_ref, place, all_ref, win_ref)
        acc_ref[...] = jnp.zeros_like(acc_ref)

        def step(pair, carry):
            grads = head_pair(g_ref, a, pair)
            bias = jnp.concatenate([bias_ref[...], bias_ref[...]], axis=1)
            scores = nt(win_ref[...], head_pair(q_ref, a, pair)) * (SCALING * LOG2E) + bias
            highest = jnp.max(scores, axis=0, keepdims=True)
            raised = jnp.exp2(scores - highest)
            total = jnp.sum(raised, axis=0, keepdims=True)
            total_ref[pl.ds(a * PAIRS + pair, 1), :] = highest + jnp.log2(total)
            probs = (raised * (1.0 / total)).astype(bf16)
            acc_ref[...] += nn(probs, grads)
            return carry

        lax.fori_loop(0, PAIRS, step, 0)
        add_window(table_ref, place, acc_ref, sum_ref)
    o0[...] = sum_ref[0:512, :]
    for i, out in enumerate((o1, o2, o3)):
        out[...] = sum_ref[512 * (i + 1) : 512 * (i + 2), :].astype(bf16)


def key_side_kernel(
    table_ref, doc_ref, q_ref, g_ref, total_ref, term_ref, k0, k1, k2, k3, v0, v1, v2, v3,
    dq_ref, o0, o1, o2, o3, allk_ref, allv_ref, wink_ref, winv_ref, bias_ref, acc_ref, sum_ref,
):
    join((k0, k1, k2, k3), allk_ref)
    join((v0, v1, v2, v3), allv_ref)
    sum_ref[...] = jnp.zeros_like(sum_ref)
    for a in range(2):
        place = table_ref[16 + a]
        fill_bias(place, doc_ref, bias_ref)
        fill_window(table_ref, place, allk_ref, wink_ref)
        fill_window(table_ref, place, allv_ref, winv_ref)
        acc_ref[...] = jnp.zeros_like(acc_ref)

        def step(pair, carry):
            row = pl.ds(a * PAIRS + pair, 1)
            query = head_pair(q_ref, a, pair)
            bias = jnp.concatenate([bias_ref[...], bias_ref[...]], axis=1)
            scores = nt(wink_ref[...], query) * (SCALING * LOG2E) + bias
            probs = jnp.exp2(scores - total_ref[row, :])
            dprobs = nt(winv_ref[...], head_pair(g_ref, a, pair))
            dscores = (probs * (dprobs - term_ref[row, :])).astype(bf16)
            acc_ref[...] += nn(dscores, query)
            dquery = (tn(dscores, wink_ref[...]) * SCALING).astype(bf16)
            rows = slice(a * BLOCK, (a + 1) * BLOCK)
            dq_ref[rows, pl.ds(pl.multiple_of(pair * 256, 256), HEAD_SIZE)] = dquery[:BLOCK]
            dq_ref[rows, pl.ds(pl.multiple_of(pair * 256 + 128, 128), HEAD_SIZE)] = dquery[BLOCK:]
            return carry

        lax.fori_loop(0, PAIRS, step, 0)
        add_window(table_ref, place, acc_ref, sum_ref)
    o0[...] = sum_ref[0:512, :] * SCALING
    for i, out in enumerate((o1, o2, o3)):
        out[...] = (sum_ref[512 * (i + 1) : 512 * (i + 2), :] * SCALING).astype(bf16)


def project_kernel(slab_ref, ha, hb, w0, w1, w2, w3, oa, ob):
    sum_a = jnp.zeros(oa.shape, f32)
    sum_b = jnp.zeros(ob.shape, f32)
    for r, w in enumerate((w0, w1, w2, w3)):
        for i in range(4):
            cols = pl.ds(pl.multiple_of(slab_ref[r * 4 + i] * SLAB, BLOCK), SLAB)
            weight = w[i * SLAB : (i + 1) * SLAB, :]
            sum_a = sum_a + nn(ha[:, cols], weight)
            sum_b = sum_b + nn(hb[:, cols], weight)
    oa[...] = sum_a
    ob[...] = sum_b


def weight_kernel(slab_ref, ha, hb, va, vb, o0, o1, o2, o3):
    for r, out in enumerate((o0, o1, o2, o3)):
        for i in range(4):
            cols = pl.ds(pl.multiple_of(slab_ref[r * 4 + i] * SLAB, BLOCK), SLAB)
            block = tn(va[...], ha[:, cols]) + tn(vb[...], hb[:, cols])
            out[:, i * SLAB : (i + 1) * SLAB] = block.astype(out.dtype)


SMEM = pl.BlockSpec(memory_space=pltpu.SMEM)
VMEM = pl.BlockSpec(memory_space=pltpu.VMEM)


def call(kernel, outs, ins, scratch=(), flops=0, moved_bytes=0, exps=0, smem=1, limit=40):
    return pl.pallas_call(
        kernel,
        out_shape=tuple(jax.ShapeDtypeStruct(s, d) for s, d in outs),
        in_specs=[SMEM] * smem + [VMEM] * (len(ins) - smem),
        out_specs=tuple(VMEM for _ in outs),
        scratch_shapes=[pltpu.VMEM(s, d) for s, d in scratch],
        compiler_params=pltpu.CompilerParams(vmem_limit_bytes=limit * 1024 * 1024),
        cost_estimate=pl.CostEstimate(flops=flops, bytes_accessed=moved_bytes, transcendentals=exps),
    )(*ins)


def gathered(value):
    both = jnp.concatenate([value, x_swap(value)], axis=0)
    return (both, z_step(both, -1), z_step(both, -2), z_step(both, -3))


def summed(own, one, two, three):
    rows = own.shape[0] // 2
    total = (
        own
        + z_step(one, 1).astype(f32)
        + z_step(two, 2).astype(f32)
        + z_step(three, 3).astype(f32)
    )
    return total[:rows] + x_swap(total[rows:].astype(bf16)).astype(f32)


def local(
    hidden_in,
    queries,
    rotary_key_rows,
    value_projection,
    output_gradient,
    attended,
    doc_ids,
    block_place,
):
    dp = lax.axis_index("dp")
    ctx = lax.axis_index("ctx")
    x_hi, core = dp // 2, dp % 2
    x_lo, z = ctx // 4, ctx % 4
    x = x_hi * 2 + x_lo
    rows = queries.shape[1]
    grad_scale = float(rows * 32) ** (-0.5)
    query, grad, saved = queries[0], output_gradient[0], attended[0]
    docs = doc_ids[0].reshape(16, BLOCK)
    placing = block_place[0]

    stored = jnp.arange(16, dtype=jnp.int32)
    owner = stored // 2
    lies = ((owner % 4 - z) % 4) * 4 + ((owner // 4 + x_lo) % 2) * 2 + stored % 2
    at_place = jnp.sum(jnp.where(placing[None, :] == stored[:, None], lies[None, :], 0), axis=1)
    mine = jnp.sum(jnp.where(stored[None, :] == (2 * ctx + jnp.arange(2))[:, None], placing[None, :], 0), axis=1)
    table = jnp.concatenate([at_place, mine])

    outer, inner = jnp.arange(16, dtype=jnp.int32) // 4, jnp.arange(16, dtype=jnp.int32) % 4
    slab_x = (x + jnp.where(core == 0, outer, inner)) % 4
    slab_z = (z + jnp.where(core == 0, inner, outer)) % 4
    slabs = (slab_x // 2) * 8 + (slab_x % 2) * 4 + slab_z

    keys = gathered(rotary_key_rows[0])

    first = jnp.concatenate(
        [value_projection] + [first_step(value_projection, -i) for i in (1, 2, 3)], axis=0
    )
    weights = (first,) + tuple(second_step(first, -i) for i in (1, 2, 3))

    turned = lax.ppermute(
        value_projection, ("dp", "head"), [(i * 4 + j, j * 4 + i) for i in range(4) for j in range(4)]
    )
    own_rows = lax.all_gather(turned, ("dp", "ctx"), axis=0, tiled=True).reshape(4, 3072, HEAD_SIZE)

    quarters = hidden_in[0].reshape(rows, 2, 2, 3072)
    ha = lax.dynamic_index_in_dim(quarters, core, 2, keepdims=False).reshape(rows, 6144)
    hb = core_swap(
        lax.dynamic_index_in_dim(quarters, 1 - core, 2, keepdims=False).reshape(rows, 6144)
    )

    (terms,) = call(row_terms_kernel, [((12, 256), f32)], [grad, saved], smem=0, moved_bytes=1 << 21)

    window = ((SPAN, HEAD_SIZE), bf16)
    whole = ((2048, HEAD_SIZE), bf16)
    sums = [((SPAN, BLOCK), f32), ((SPAN, HEAD_SIZE), f32), ((2048, HEAD_SIZE), f32)]
    parts_out = [((512, HEAD_SIZE), f32)] + [((512, HEAD_SIZE), bf16)] * 3
    dots = 2 * 12 * 256 * SPAN * HEAD_SIZE
    totals, *value_parts = call(
        value_side_kernel,
        [((12, 256), f32)] + parts_out,
        [table, docs, query, grad, *keys],
        scratch=[whole, window] + sums,
        flops=2 * dots, moved_bytes=4 << 20, exps=12 * 256 * SPAN,
    )
    value_grads = summed(*value_parts).astype(bf16)
    sibling_grads = core_swap(value_grads)

    part_a, part_b = call(
        project_kernel,
        [((rows, HEAD_SIZE), f32)] * 2,
        [slabs, ha, hb, *weights],
        flops=2 * 512 * 6144 * 128, moved_bytes=8 << 20,
    )
    values = gathered((part_a + core_swap(part_b)).astype(bf16))

    w_parts = call(
        weight_kernel,
        [((HEAD_SIZE, 1536), f32)] + [((HEAD_SIZE, 1536), bf16)] * 3,
        [slabs, ha, hb, value_grads, sibling_grads],
        flops=2 * 512 * 6144 * 128, moved_bytes=8 << 20,
    )
    w_sum = w_parts[0]
    for i in (1, 2, 3):
        w_sum = w_sum + second_step(w_parts[i], i).astype(f32)
    w_total = w_sum[:, :SLAB]
    for i in (1, 2, 3):
        w_total = w_total + first_step(w_sum[:, i * SLAB : (i + 1) * SLAB].astype(bf16), i).astype(f32)
    weight_grad = (w_total * grad_scale).T

    head = lax.axis_index("head")
    every = jnp.zeros((4, rows, HEAD_SIZE), bf16)
    every = lax.dynamic_update_index_in_dim(every, value_grads, head, 0)
    for i in (1, 2, 3):
        got = lax.ppermute(value_grads, "head", [(s, (s - i) % 4) for s in range(4)])
        every = lax.dynamic_update_index_in_dim(every, got, (head + i) % 4, 0)
    input_grad = jnp.einsum("hrk,hnk->rn", every, own_rows, preferred_element_type=f32).astype(bf16)

    dquery, *key_parts = call(
        key_side_kernel,
        [((rows, 1536), bf16)] + parts_out,
        [table, docs, query, grad, totals, terms, *keys, *values],
        scratch=[whole, whole, window, window] + sums,
        flops=4 * dots, moved_bytes=6 << 20, exps=12 * 256 * SPAN,
    )
    key_grads = summed(*key_parts).astype(bf16)
    return dquery[None], key_grads[None], input_grad[None], weight_grad


def solution(mesh):
    in_specs = (
        P("dp", "ctx", None),
        P("dp", "ctx", "head"),
        P("dp", "ctx", "head"),
        P(("dp", "ctx"), "head"),
        P("dp", "ctx", "head"),
        P("dp", "ctx", "head"),
        P("dp", None),
        P("dp", None),
    )
    out_specs = (
        P("dp", "ctx", "head"),
        P("dp", "ctx", "head"),
        P("dp", "ctx", "head"),
        P(("dp", "ctx"), "head"),
    )
    return jax.shard_map(local, mesh=mesh, in_specs=in_specs, out_specs=out_specs, check_vma=False)
```

```python
import jax
import jax.numpy as jnp
from jax import lax
from jax.experimental import pallas as pl
from jax.experimental.pallas import tpu as pltpu
from jax.sharding import PartitionSpec as P

HEAD_SIZE = 128
QUERY_PER_KEY = 12
PAIRS = QUERY_PER_KEY // 2
BLOCK = 128
WINDOW = 9
SPAN = WINDOW * BLOCK
SLAB = 384
QUARTER = 3072
MASKED = -1e30
LOG2E = 1.4426950408889634
SCALING = float(HEAD_SIZE) ** (-0.5)
f32 = jnp.float32
bf16 = jnp.bfloat16


def place_of(index):
    dp, ctx = divmod(index, 8)
    x_hi, core = divmod(dp, 2)
    x_lo, z = divmod(ctx, 4)
    return x_hi * 2 + x_lo, z, core


def index_of(x, z, core):
    x_hi, x_lo = divmod(x % 4, 2)
    return (x_hi * 2 + core) * 8 + x_lo * 4 + z % 4


def moved(value, where):
    pairs = [(i, index_of(*where(*place_of(i)))) for i in range(32)]
    return lax.ppermute(value, ("dp", "ctx"), pairs)


def core_swap(value):
    return moved(value, lambda x, z, c: (x, z, 1 - c))


def x_swap(value):
    return moved(value, lambda x, z, c: (x ^ 1, z, c))


def z_step(value, by):
    return moved(value, lambda x, z, c: (x, z + by, c))


def first_step(value, by):
    return moved(value, lambda x, z, c: (x, z + by, c) if c == 0 else (x + by, z, c))


def second_step(value, by):
    return moved(value, lambda x, z, c: (x + by, z, c) if c == 0 else (x, z + by, c))


def nt(a, b):
    return lax.dot_general(a, b, (((1,), (1,)), ((), ())), preferred_element_type=f32)


def nn(a, b):
    return lax.dot_general(a, b, (((1,), (0,)), ((), ())), preferred_element_type=f32)


def tn(a, b):
    return lax.dot_general(a, b, (((0,), (0,)), ((), ())), preferred_element_type=f32)


def row_terms_kernel(grad_ref, saved_ref, out_ref):
    for a in range(2):
        rows = slice(a * BLOCK, (a + 1) * BLOCK)
        for h in range(QUERY_PER_KEY):
            cols = slice(h * HEAD_SIZE, (h + 1) * HEAD_SIZE)
            product = grad_ref[rows, cols].astype(f32) * saved_ref[rows, cols].astype(f32)
            at = a * QUERY_PER_KEY + h
            out_ref[at : at + 1, :] = jnp.sum(product.T, axis=0, keepdims=True)


def pick_kernel(table_ref, in_ref, out_ref):
    out_ref[...] = in_ref[...]


def fill_bias(place, doc_ref, bias_ref):
    docs = doc_ref[...]
    own = doc_ref[pl.ds(place, 1), :]
    start = jnp.zeros((1, BLOCK), f32)
    for d in range(1, 6):
        held = jnp.sum(jnp.where(docs == d - 1, 1.0, 0.0), axis=(0, 1), keepdims=True)
        start = start + jnp.where(own >= d, held, 0.0)
    start = start.astype(jnp.int32)
    query = place * BLOCK + lax.broadcasted_iota(jnp.int32, (1, BLOCK), 1)
    key = (place - (WINDOW - 1)) * BLOCK + lax.broadcasted_iota(jnp.int32, (SPAN, 1), 0)
    bias_ref[...] = jnp.where((key >= start) & (key <= query), 0.0, MASKED)


def fill_window(table_ref, place, parts, win_ref):
    for j in range(WINDOW):
        block = table_ref[jnp.maximum(place - (WINDOW - 1) + j, 0)]
        win_ref[j * BLOCK : (j + 1) * BLOCK, :] = parts[pl.ds(pl.multiple_of(block * BLOCK, BLOCK), BLOCK), :]


def join(parts, all_ref):
    rows = parts[0].shape[0]
    for i, part in enumerate(parts):
        all_ref[i * rows : (i + 1) * rows, :] = part[...]


def stacked(ref, a, pair):
    rows = slice(a * BLOCK, (a + 1) * BLOCK)
    one = ref[rows, pair * 256 : pair * 256 + 128]
    two = ref[rows, pair * 256 + 128 : pair * 256 + 256]
    return jnp.concatenate([one, two], axis=0)


def beside(ref, a, pair):
    at = a * QUERY_PER_KEY + 2 * pair
    return jnp.concatenate([ref[at : at + 1, :], ref[at + 1 : at + 2, :]], axis=1)


def add_window(table_ref, place, win_ref, sum_ref):
    for j in range(WINDOW):
        block = table_ref[jnp.maximum(place - (WINDOW - 1) + j, 0)]
        at = pl.ds(pl.multiple_of(block * BLOCK, BLOCK), BLOCK)
        sum_ref[at, :] += win_ref[j * BLOCK : (j + 1) * BLOCK, :]


def value_side_kernel(
    table_ref, doc_ref, q_ref, g_ref, k0, k1, k2, k3,
    total_ref, o0, o1, o2, o3,
    all_ref, win_ref, bias_ref, score_ref, raised_ref, scaled_ref, acc_ref, sum_ref,
):
    join((k0, k1, k2, k3), all_ref)
    sum_ref[...] = jnp.zeros_like(sum_ref)
    for a in range(2):
        place = table_ref[16 + a]
        fill_bias(place, doc_ref, bias_ref)
        fill_window(table_ref, place, all_ref, win_ref)
        for pair in range(PAIRS):
            cols = slice(pair * 256, (pair + 1) * 256)
            products = nt(win_ref[...], stacked(q_ref, a, pair))
            highest = None
            for j in range(WINDOW):
                keys = slice(j * BLOCK, (j + 1) * BLOCK)
                bias = jnp.concatenate([bias_ref[keys, :]] * 2, axis=1)
                scores = products[keys] * (SCALING * LOG2E) + bias
                score_ref[keys, :] = scores
                highest = scores if highest is None else jnp.maximum(highest, scores)
            highest = jnp.max(highest, axis=0, keepdims=True)
            total = None
            for j in range(WINDOW):
                keys = slice(j * BLOCK, (j + 1) * BLOCK)
                raised = jnp.exp2(score_ref[keys, :] - highest)
                total = raised if total is None else total + raised
                raised_ref[keys, cols] = raised.astype(bf16)
            total = jnp.sum(total, axis=0, keepdims=True)
            log_total = highest + jnp.log2(total)
            share = 1.0 / total
            for half in range(2):
                h = 2 * pair + half
                lanes = slice(half * BLOCK, (half + 1) * BLOCK)
                at = a * QUERY_PER_KEY + h
                total_ref[at : at + 1, :] = log_total[:, lanes]
                factor = jnp.broadcast_to(share[:, lanes], (BLOCK, BLOCK)).T
                grads = g_ref[a * BLOCK : (a + 1) * BLOCK, h * HEAD_SIZE : (h + 1) * HEAD_SIZE]
                scaled_ref[h * BLOCK : (h + 1) * BLOCK, :] = (grads.astype(f32) * factor).astype(bf16)
        acc_ref[...] = nn(raised_ref[...], scaled_ref[...])
        add_window(table_ref, place, acc_ref, sum_ref)
    o0[...] = sum_ref[0:512, :]
    for i, out in enumerate((o1, o2, o3)):
        out[...] = sum_ref[512 * (i + 1) : 512 * (i + 2), :].astype(bf16)


def key_side_kernel(
    table_ref, doc_ref, q_ref, g_ref, total_ref, term_ref, k0, k1, k2, k3, v0, v1, v2, v3,
    dq_ref, o0, o1, o2, o3,
    allk_ref, allv_ref, wink_ref, winv_ref, bias_ref, ds_ref, qs_ref, acc_ref, sum_ref,
):
    join((k0, k1, k2, k3), allk_ref)
    join((v0, v1, v2, v3), allv_ref)
    sum_ref[...] = jnp.zeros_like(sum_ref)
    for a in range(2):
        place = table_ref[16 + a]
        fill_bias(place, doc_ref, bias_ref)
        fill_window(table_ref, place, allk_ref, wink_ref)
        fill_window(table_ref, place, allv_ref, winv_ref)
        for pair in range(PAIRS):
            cols = slice(pair * 256, (pair + 1) * 256)
            query = stacked(q_ref, a, pair)
            qs_ref[cols, :] = query
            products = nt(wink_ref[...], query)
            dprobs = nt(winv_ref[...], stacked(g_ref, a, pair))
            log_total = beside(total_ref, a, pair)
            terms = beside(term_ref, a, pair)
            for j in range(WINDOW):
                keys = slice(j * BLOCK, (j + 1) * BLOCK)
                bias = jnp.concatenate([bias_ref[keys, :]] * 2, axis=1)
                probs = jnp.exp2(products[keys] * (SCALING * LOG2E) + bias - log_total)
                ds_ref[keys, cols] = (probs * (dprobs[keys] - terms)).astype(bf16)
        dquery = tn(wink_ref[...], ds_ref[...]) * SCALING
        for h in range(QUERY_PER_KEY):
            dq_ref[a * BLOCK : (a + 1) * BLOCK, h * HEAD_SIZE : (h + 1) * HEAD_SIZE] = (
                dquery[:, h * BLOCK : (h + 1) * BLOCK].T.astype(bf16)
            )
        acc_ref[...] = nn(ds_ref[...], qs_ref[...])
        add_window(table_ref, place, acc_ref, sum_ref)
    o0[...] = sum_ref[0:512, :] * SCALING
    for i, out in enumerate((o1, o2, o3)):
        out[...] = (sum_ref[512 * (i + 1) : 512 * (i + 2), :] * SCALING).astype(bf16)


def own_half_copies(table_ref, hidden, half_ref, sems):
    return [
        pltpu.make_async_copy(
            hidden.at[:, pl.ds(pl.multiple_of(table_ref[16 + p] * QUARTER, BLOCK), QUARTER)],
            half_ref.at[:, p * QUARTER : (p + 1) * QUARTER],
            sems.at[p],
        )
        for p in range(2)
    ]


def project_kernel(table_ref, hidden, hb, w0, w1, w2, w3, oa, ob, lower, upper, ha_ref, all_ref, sems):
    copies = own_half_copies(table_ref, hidden, ha_ref, sems)
    for copy in copies:
        copy.start()
    for r, w in enumerate((w0, w1, w2, w3)):
        for i in range(4):
            at = pl.multiple_of(table_ref[r * 4 + i] * SLAB, BLOCK)
            all_ref[pl.ds(at, SLAB), :] = w[i * SLAB : (i + 1) * SLAB, :]
    lower[...] = all_ref[:QUARTER, :]
    upper[...] = all_ref[QUARTER:, :]
    ob[...] = nn(hb[...], all_ref[...])
    for copy in copies:
        copy.wait()
    oa[...] = nn(ha_ref[...], all_ref[...])


def weight_kernel(table_ref, hidden, hb, va, vb, o0, o1, o2, o3, ha_ref, sems):
    copies = own_half_copies(table_ref, hidden, ha_ref, sems)
    for copy in copies:
        copy.start()
    one, two = va[...].T, vb[...].T
    for copy in copies:
        copy.wait()
    for r, out in enumerate((o0, o1, o2, o3)):
        for i in range(4):
            cols = pl.ds(pl.multiple_of(table_ref[r * 4 + i] * SLAB, BLOCK), SLAB)
            block = nn(one, ha_ref[:, cols]) + nn(two, hb[:, cols])
            out[:, i * SLAB : (i + 1) * SLAB] = block.astype(out.dtype)


def input_kernel(table_ref, g0, g1, g2, g3, *refs):
    mine, other, out, rows_ref, sems = refs[:4], refs[4:8], refs[8], refs[9], refs[10]
    for choice, pieces in ((1, mine), (0, other)):

        @pl.when(table_ref[18] == choice)
        def _(pieces=pieces):
            copies = [
                pltpu.make_async_copy(p, rows_ref.at[:, d * BLOCK : (d + 1) * BLOCK], sems.at[d])
                for d, p in enumerate(pieces)
            ]
            for copy in copies:
                copy.start()
            for copy in copies:
                copy.wait()

    grads = jnp.concatenate([g0[...], g1[...], g2[...], g3[...]], axis=1)
    for part in range(4):
        cols = slice(part * 768, (part + 1) * 768)
        out[:, cols] = nt(grads, rows_ref[cols, :]).astype(bf16)


SMEM = pl.BlockSpec(memory_space=pltpu.SMEM)
VMEM = pl.BlockSpec(memory_space=pltpu.VMEM)


def call(kernel, outs, ins, scratch=(), flops=0, moved_bytes=0, exps=0, smem=1, anys=(), limit=40):
    any_spec = pl.BlockSpec(memory_space=pl.ANY)
    specs = [SMEM] * smem + [any_spec if i in anys else VMEM for i in range(smem, len(ins))]
    return pl.pallas_call(
        kernel,
        out_shape=tuple(jax.ShapeDtypeStruct(s, d) for s, d in outs),
        in_specs=specs,
        out_specs=tuple(VMEM for _ in outs),
        scratch_shapes=[s if not isinstance(s, tuple) else pltpu.VMEM(*s) for s in scratch],
        compiler_params=pltpu.CompilerParams(vmem_limit_bytes=limit * 1024 * 1024),
        cost_estimate=pl.CostEstimate(flops=flops, bytes_accessed=moved_bytes, transcendentals=exps),
    )(*ins)


def gathered(value):
    both = jnp.concatenate([value, x_swap(value)], axis=0)
    return (both, z_step(both, -1), z_step(both, -2), z_step(both, -3))


def summed(own, one, two, three):
    rows = own.shape[0] // 2
    total = (
        own
        + z_step(one, 1).astype(f32)
        + z_step(two, 2).astype(f32)
        + z_step(three, 3).astype(f32)
    )
    return total[:rows] + x_swap(total[rows:].astype(bf16)).astype(f32)


def local(
    hidden_in,
    queries,
    rotary_key_rows,
    value_projection,
    output_gradient,
    attended,
    doc_ids,
    block_place,
):
    dp = lax.axis_index("dp")
    ctx = lax.axis_index("ctx")
    x_hi, core = dp // 2, dp % 2
    x_lo, z = ctx // 4, ctx % 4
    x = x_hi * 2 + x_lo
    rows = queries.shape[1]
    grad_scale = float(rows * 32) ** (-0.5)
    query, grad, saved = queries[0], output_gradient[0], attended[0]
    docs = doc_ids[0].reshape(16, BLOCK)
    placing = block_place[0]

    stored = jnp.arange(16, dtype=jnp.int32)
    owner = stored // 2
    lies = ((owner % 4 - z) % 4) * 4 + ((owner // 4 + x_lo) % 2) * 2 + stored % 2
    at_place = jnp.sum(jnp.where(placing[None, :] == stored[:, None], lies[None, :], 0), axis=1)
    mine = jnp.sum(jnp.where(stored[None, :] == (2 * ctx + jnp.arange(2))[:, None], placing[None, :], 0), axis=1)
    table = jnp.concatenate([at_place, mine])

    head = lax.axis_index("head")

    def quarters_of(core):
        lead = ((head + (head % 2 != core)) % 4) // 2
        return jnp.stack([2 * lead + core, 2 * (1 - lead) + core]), lead

    own_quarters, lead = quarters_of(core)
    other_quarters, _ = quarters_of(1 - core)

    outer, inner = jnp.arange(16, dtype=jnp.int32) // 4, jnp.arange(16, dtype=jnp.int32) % 4
    slab_x = (x + jnp.where(core == 0, outer, inner)) % 4
    slab_z = (z + jnp.where(core == 0, inner, outer)) % 4
    slabs = ((slab_x // 2 + lead) % 2) * 8 + (slab_x % 2) * 4 + slab_z
    has_rows = (head % 2 == core).astype(jnp.int32)
    slabs = jnp.concatenate([slabs, own_quarters, has_rows[None]]).astype(jnp.int32)

    keys = gathered(rotary_key_rows[0])

    first = jnp.concatenate(
        [value_projection] + [first_step(value_projection, -i) for i in (1, 2, 3)], axis=0
    )
    weights = (first,) + tuple(second_step(first, -i) for i in (1, 2, 3))

    hidden = hidden_in[0]
    picked = pl.pallas_call(
        pick_kernel,
        grid_spec=pltpu.PrefetchScalarGridSpec(
            num_scalar_prefetch=1,
            grid=(4,),
            in_specs=[pl.BlockSpec((rows, QUARTER // 2), lambda i, t: (0, t[i // 2] * 2 + i % 2))],
            out_specs=pl.BlockSpec((rows, QUARTER // 2), lambda i, t: (0, i)),
        ),
        out_shape=jax.ShapeDtypeStruct((rows, 2 * QUARTER), bf16),
        cost_estimate=pl.CostEstimate(flops=0, bytes_accessed=6 << 20, transcendentals=0),
    )(other_quarters.astype(jnp.int32), hidden)
    hb = core_swap(picked)

    (terms,) = call(row_terms_kernel, [((24, 128), f32)], [grad, saved], smem=0, moved_bytes=1 << 21)

    window = ((SPAN, HEAD_SIZE), bf16)
    whole = ((2048, HEAD_SIZE), bf16)
    bias = ((SPAN, BLOCK), f32)
    square = ((SPAN, 1536), bf16)
    stack = ((1536, HEAD_SIZE), bf16)
    sums = [((SPAN, HEAD_SIZE), f32), ((2048, HEAD_SIZE), f32)]
    parts_out = [((512, HEAD_SIZE), f32)] + [((512, HEAD_SIZE), bf16)] * 3
    dots = 2 * 12 * 256 * SPAN * HEAD_SIZE
    totals, *value_parts = call(
        value_side_kernel,
        [((24, 128), f32)] + parts_out,
        [table, docs, query, grad, *keys],
        scratch=[whole, window, bias, ((SPAN, 256), f32), square, stack] + sums,
        flops=4 * dots, moved_bytes=4 << 20, exps=12 * 256 * SPAN,
    )
    value_grads = summed(*value_parts).astype(bf16)
    sibling_grads = core_swap(value_grads)

    half = ((rows, 2 * QUARTER), bf16)
    sems = pltpu.SemaphoreType.DMA((4,))
    part_a, part_b, lower, upper = call(
        project_kernel,
        [((rows, HEAD_SIZE), f32)] * 2 + [((QUARTER, HEAD_SIZE), bf16)] * 2,
        [slabs, hidden, hb, *weights],
        scratch=[half, ((2 * QUARTER, HEAD_SIZE), bf16), sems], anys=(1,),
        flops=2 * 512 * 6144 * 128, moved_bytes=10 << 20,
    )
    values = gathered((part_a + core_swap(part_b)).astype(bf16))

    def along_y(value, by):
        pairs = []
        for s in range(4):
            for dp_at in range(4):
                if (s + by) % 2 == dp_at % 2:
                    pairs.append((dp_at * 4 + s, dp_at * 4 + (s + by) % 4))
        return lax.ppermute(value, ("dp", "head"), pairs)

    own_rows = [lower, along_y(lower, 1), along_y(upper, 2), along_y(upper, 3)]
    swapped_rows = [core_swap(r) for r in own_rows]

    w_parts = call(
        weight_kernel,
        [((HEAD_SIZE, 1536), f32)] + [((HEAD_SIZE, 1536), bf16)] * 3,
        [slabs, hidden, hb, value_grads, sibling_grads],
        scratch=[half, sems], anys=(1,),
        flops=2 * 512 * 6144 * 128, moved_bytes=8 << 20,
    )
    w_sum = w_parts[0]
    for i in (1, 2, 3):
        w_sum = w_sum + second_step(w_parts[i], i).astype(f32)
    w_total = w_sum[:, :SLAB]
    for i in (1, 2, 3):
        w_total = w_total + first_step(w_sum[:, i * SLAB : (i + 1) * SLAB].astype(bf16), i).astype(f32)
    weight_grad = (w_total * grad_scale).T

    every = [value_grads] + [
        lax.ppermute(value_grads, "head", [(s, (s + i) % 4) for s in range(4)]) for i in (1, 2, 3)
    ]
    (input_grad,) = call(
        input_kernel,
        [((rows, QUARTER), bf16)],
        [slabs, *every, *own_rows, *swapped_rows],
        scratch=[((QUARTER, 512), bf16), sems], anys=tuple(range(5, 13)),
        flops=2 * 256 * 512 * 3072, moved_bytes=5 << 20,
    )

    dquery, *key_parts = call(
        key_side_kernel,
        [((rows, 1536), bf16)] + parts_out,
        [table, docs, query, grad, totals, terms, *keys, *values],
        scratch=[whole, whole, window, window, bias, square, stack] + sums,
        flops=8 * dots, moved_bytes=6 << 20, exps=12 * 256 * SPAN,
    )
    key_grads = summed(*key_parts).astype(bf16)
    return dquery[None], key_grads[None], input_grad[None], weight_grad


def solution(mesh):
    in_specs = (
        P("dp", "ctx", None),
        P("dp", "ctx", "head"),
        P("dp", "ctx", "head"),
        P(("dp", "ctx"), "head"),
        P("dp", "ctx", "head"),
        P("dp", "ctx", "head"),
        P("dp", None),
        P("dp", None),
    )
    out_specs = (
        P("dp", "ctx", "head"),
        P("dp", "ctx", "head"),
        P("dp", "ctx", "head"),
        P(("dp", "ctx"), "head"),
    )
    return jax.shard_map(local, mesh=mesh, in_specs=in_specs, out_specs=out_specs, check_vma=False)
```

```python
import functools

import jax
import jax.numpy as jnp
from jax import lax
from jax.experimental import pallas as pl
from jax.experimental.pallas import tpu as pltpu
from jax.sharding import PartitionSpec as P

HEAD_SIZE = 128
QUERY_PER_KEY = 12
PAIRS = QUERY_PER_KEY // 2
BLOCK = 128
WINDOW = 9
SPAN = WINDOW * BLOCK
SLAB = 384
QUARTER = 3072
HALF = QUARTER // 2
COST_UNIT = 3 << 20
MASKED = -1e30
LOG2E = 1.4426950408889634
SCALING = float(HEAD_SIZE) ** (-0.5)
f32 = jnp.float32
bf16 = jnp.bfloat16


def place_of(index):
    dp, ctx = divmod(index, 8)
    x_hi, core = divmod(dp, 2)
    x_lo, z = divmod(ctx, 4)
    return x_hi * 2 + x_lo, z, core


def index_of(x, z, core):
    x_hi, x_lo = divmod(x % 4, 2)
    return (x_hi * 2 + core) * 8 + x_lo * 4 + z % 4


def moved(value, where):
    pairs = [(i, index_of(*where(*place_of(i)))) for i in range(32)]
    return lax.ppermute(value, ("dp", "ctx"), pairs)


def core_swap(value):
    return moved(value, lambda x, z, c: (x, z, 1 - c))


def x_swap(value):
    return moved(value, lambda x, z, c: (x ^ 1, z, c))


def z_with(value, bits):
    return moved(value, lambda x, z, c: (x, z ^ bits, c))


def first_with(value, bits):
    return moved(value, lambda x, z, c: (x, z ^ bits, c) if c == 0 else (x ^ bits, z, c))


def second_with(value, bits):
    return moved(value, lambda x, z, c: (x ^ bits, z, c) if c == 0 else (x, z ^ bits, c))


def y_with(value, bits):
    return lax.ppermute(value, "head", [(y, y ^ bits) for y in range(4)])


def nt(a, b):
    return lax.dot_general(a, b, (((1,), (1,)), ((), ())), preferred_element_type=f32)


def nn(a, b):
    return lax.dot_general(a, b, (((1,), (0,)), ((), ())), preferred_element_type=f32)


def tn(a, b):
    return lax.dot_general(a, b, (((0,), (0,)), ((), ())), preferred_element_type=f32)


def row_terms_kernel(grad_ref, saved_ref, out_ref):
    for a in range(2):
        rows = slice(a * BLOCK, (a + 1) * BLOCK)
        for h in range(QUERY_PER_KEY):
            cols = slice(h * HEAD_SIZE, (h + 1) * HEAD_SIZE)
            product = grad_ref[rows, cols].astype(f32) * saved_ref[rows, cols].astype(f32)
            at = a * QUERY_PER_KEY + h
            out_ref[at : at + 1, :] = jnp.sum(product.T, axis=0, keepdims=True)


def join_kernel(*refs):
    join(refs[:-1], refs[-1])


def fold_kernel(scale, own, one, two, three, out):
    total = own[...] + one[...].astype(f32) + two[...].astype(f32) + three[...].astype(f32)
    out[...] = (total * scale).T


def fill_bias(place, doc_ref, bias_ref):
    docs = doc_ref[...]
    own = doc_ref[pl.ds(place, 1), :]
    start = jnp.zeros((1, BLOCK), f32)
    for d in range(1, 6):
        held = jnp.sum(jnp.where(docs == d - 1, 1.0, 0.0), axis=(0, 1), keepdims=True)
        start = start + jnp.where(own >= d, held, 0.0)
    start = start.astype(jnp.int32)
    query = place * BLOCK + lax.broadcasted_iota(jnp.int32, (1, BLOCK), 1)
    key = (place - (WINDOW - 1)) * BLOCK + lax.broadcasted_iota(jnp.int32, (SPAN, 1), 0)
    bias_ref[...] = jnp.where((key >= start) & (key <= query), 0.0, MASKED)


def fill_window(table_ref, place, parts, win_ref):
    for j in range(WINDOW):
        block = table_ref[jnp.maximum(place - (WINDOW - 1) + j, 0)]
        win_ref[j * BLOCK : (j + 1) * BLOCK, :] = parts[pl.ds(pl.multiple_of(block * BLOCK, BLOCK), BLOCK), :]


def join(parts, all_ref):
    rows = parts[0].shape[0]
    for i, part in enumerate(parts):
        all_ref[i * rows : (i + 1) * rows, :] = part[...]


def stacked(ref, a, pair):
    rows = slice(a * BLOCK, (a + 1) * BLOCK)
    one = ref[rows, pair * 256 : pair * 256 + 128]
    two = ref[rows, pair * 256 + 128 : pair * 256 + 256]
    return jnp.concatenate([one, two], axis=0)


def beside(ref, a, pair):
    at = a * QUERY_PER_KEY + 2 * pair
    return jnp.concatenate([ref[at : at + 1, :], ref[at + 1 : at + 2, :]], axis=1)


def add_window(table_ref, place, win_ref, sum_ref):
    for j in range(WINDOW):
        block = table_ref[jnp.maximum(place - (WINDOW - 1) + j, 0)]
        at = pl.ds(pl.multiple_of(block * BLOCK, BLOCK), BLOCK)
        sum_ref[at, :] += win_ref[j * BLOCK : (j + 1) * BLOCK, :]


def value_side_kernel(
    table_ref, doc_ref, q_ref, g_ref, k0, k1, k2, k3,
    total_ref, o0, o1, o2, o3,
    all_ref, win_ref, bias_ref, score_ref, raised_ref, scaled_ref, acc_ref, sum_ref,
):
    join((k0, k1, k2, k3), all_ref)
    sum_ref[...] = jnp.zeros_like(sum_ref)
    for a in range(2):
        place = table_ref[16 + a]
        fill_bias(place, doc_ref, bias_ref)
        fill_window(table_ref, place, all_ref, win_ref)
        for pair in range(PAIRS):
            cols = slice(pair * 256, (pair + 1) * 256)
            products = nt(win_ref[...], stacked(q_ref, a, pair))
            highest = None
            for j in range(WINDOW):
                keys = slice(j * BLOCK, (j + 1) * BLOCK)
                bias = jnp.concatenate([bias_ref[keys, :]] * 2, axis=1)
                scores = products[keys] * (SCALING * LOG2E) + bias
                score_ref[keys, :] = scores
                highest = scores if highest is None else jnp.maximum(highest, scores)
            highest = jnp.max(highest, axis=0, keepdims=True)
            total = None
            for j in range(WINDOW):
                keys = slice(j * BLOCK, (j + 1) * BLOCK)
                raised = jnp.exp2(score_ref[keys, :] - highest)
                total = raised if total is None else total + raised
                raised_ref[keys, cols] = raised.astype(bf16)
            total = jnp.sum(total, axis=0, keepdims=True)
            log_total = highest + jnp.log2(total)
            share = 1.0 / total
            for half in range(2):
                h = 2 * pair + half
                lanes = slice(half * BLOCK, (half + 1) * BLOCK)
                at = a * QUERY_PER_KEY + h
                total_ref[at : at + 1, :] = log_total[:, lanes]
                factor = jnp.broadcast_to(share[:, lanes], (BLOCK, BLOCK)).T
                grads = g_ref[a * BLOCK : (a + 1) * BLOCK, h * HEAD_SIZE : (h + 1) * HEAD_SIZE]
                scaled_ref[h * BLOCK : (h + 1) * BLOCK, :] = (grads.astype(f32) * factor).astype(bf16)
        acc_ref[...] = nn(raised_ref[...], scaled_ref[...])
        add_window(table_ref, place, acc_ref, sum_ref)
    o0[...] = sum_ref[0:512, :]
    for i, out in enumerate((o1, o2, o3)):
        out[...] = sum_ref[512 * (i + 1) : 512 * (i + 2), :].astype(bf16)


def key_side_kernel(
    table_ref, doc_ref, q_ref, g_ref, total_ref, term_ref, k0, k1, k2, k3, v0, v1, v2, v3,
    dq_ref, o0, o1, o2, o3,
    allk_ref, allv_ref, wink_ref, winv_ref, bias_ref, ds_ref, qs_ref, acc_ref, sum_ref,
):
    join((k0, k1, k2, k3), allk_ref)
    join((v0, v1, v2, v3), allv_ref)
    sum_ref[...] = jnp.zeros_like(sum_ref)
    for a in range(2):
        place = table_ref[16 + a]
        fill_bias(place, doc_ref, bias_ref)
        fill_window(table_ref, place, allk_ref, wink_ref)
        fill_window(table_ref, place, allv_ref, winv_ref)
        for pair in range(PAIRS):
            cols = slice(pair * 256, (pair + 1) * 256)
            query = stacked(q_ref, a, pair)
            qs_ref[cols, :] = query
            products = nt(wink_ref[...], query)
            dprobs = nt(winv_ref[...], stacked(g_ref, a, pair))
            log_total = beside(total_ref, a, pair)
            terms = beside(term_ref, a, pair)
            for j in range(WINDOW):
                keys = slice(j * BLOCK, (j + 1) * BLOCK)
                bias = jnp.concatenate([bias_ref[keys, :]] * 2, axis=1)
                probs = jnp.exp2(products[keys] * (SCALING * LOG2E) + bias - log_total)
                ds_ref[keys, cols] = (probs * (dprobs[keys] - terms)).astype(bf16)
        dquery = tn(wink_ref[...], ds_ref[...]) * SCALING
        for h in range(QUERY_PER_KEY):
            dq_ref[a * BLOCK : (a + 1) * BLOCK, h * HEAD_SIZE : (h + 1) * HEAD_SIZE] = (
                dquery[:, h * BLOCK : (h + 1) * BLOCK].T.astype(bf16)
            )
        acc_ref[...] = nn(ds_ref[...], qs_ref[...])
        add_window(table_ref, place, acc_ref, sum_ref)
    o0[...] = sum_ref[0:512, :] * SCALING
    for i, out in enumerate((o1, o2, o3)):
        out[...] = (sum_ref[512 * (i + 1) : 512 * (i + 2), :] * SCALING).astype(bf16)


def project_kernel(
    table_ref, hidden, w0, w1, w2, w3, s0, s1, s2, s3, out, own_rows, r1, r2, r3, all_ref
):
    for k, w in enumerate((w0, w1, w2, w3, s0, s1, s2, s3)):
        for i in range(4):
            at = pl.multiple_of(table_ref[k * 4 + i] * SLAB, BLOCK)
            all_ref[pl.ds(at, SLAB), :] = w[i * SLAB : (i + 1) * SLAB, :]
    out[...] = nn(hidden[...], all_ref[...]).astype(bf16)
    own_rows[...] = all_ref[pl.ds(pl.multiple_of(table_ref[32] * QUARTER, BLOCK), QUARTER), :]
    for d, r in enumerate((r1, r2, r3)):
        r[...] = all_ref[pl.ds(pl.multiple_of(table_ref[33 + d] * HALF, BLOCK), HALF), :]


def weight_kernel(table_ref, hidden, grads, r1, r2, r3, own, other, m1, m2, m3):
    turned = grads[...].T
    for k in range(16):
        for out, at in ((other, 16 + k), (own, k)):
            cols = pl.ds(pl.multiple_of(table_ref[at] * SLAB, BLOCK), SLAB)
            block = nn(turned, hidden[:, cols])
            out[k * HEAD_SIZE : (k + 1) * HEAD_SIZE, :] = block.astype(out.dtype)
    for r, m in ((r1, m1), (r2, m2), (r3, m3)):
        m[:HALF, :] = r[...]
        m[HALF:, :] = grads[...]


def input_kernel(table_ref, grads, own, a1, a2, a3, b1, b2, b3, out, rows_ref, grads_ref, sems):
    mine = pl.multiple_of(table_ref[36] * HALF, BLOCK)
    other = pl.multiple_of((1 - table_ref[36]) * HALF, BLOCK)
    copies = [pltpu.make_async_copy(own, rows_ref.at[:, 0:BLOCK], sems.at[0])]
    for d, (a, b) in enumerate(((a1, b1), (a2, b2), (a3, b3))):
        cols = slice((d + 1) * BLOCK, (d + 2) * BLOCK)
        pieces = (
            (a.at[0:HALF, :], rows_ref.at[pl.ds(mine, HALF), cols]),
            (b.at[0:HALF, :], rows_ref.at[pl.ds(other, HALF), cols]),
            (a.at[HALF : HALF + 256, :], grads_ref.at[:, cols]),
        )
        for i, (source, target) in enumerate(pieces):
            copies.append(pltpu.make_async_copy(source, target, sems.at[3 * d + 1 + i]))
    for copy in copies:
        copy.start()
    grads_ref[:, 0:BLOCK] = grads[...]
    for copy in copies:
        copy.wait()
    for part in range(4):
        cols = slice(part * 768, (part + 1) * 768)
        out[:, cols] = nt(grads_ref[...], rows_ref[cols, :]).astype(bf16)


SMEM = pl.BlockSpec(memory_space=pltpu.SMEM)
VMEM = pl.BlockSpec(memory_space=pltpu.VMEM)


def call(kernel, outs, ins, scratch=(), cost=1, smem=1, anys=(), limit=8):
    any_spec = pl.BlockSpec(memory_space=pl.ANY)
    specs = [SMEM] * smem + [any_spec if i in anys else VMEM for i in range(smem, len(ins))]
    return pl.pallas_call(
        kernel,
        out_shape=tuple(jax.ShapeDtypeStruct(s, d) for s, d in outs),
        in_specs=specs,
        out_specs=tuple(VMEM for _ in outs),
        scratch_shapes=[s if not isinstance(s, tuple) else pltpu.VMEM(*s) for s in scratch],
        compiler_params=pltpu.CompilerParams(vmem_limit_bytes=limit * 1024 * 1024),
        cost_estimate=pl.CostEstimate(
            flops=0, bytes_accessed=int(cost * COST_UNIT), transcendentals=0
        ),
    )(*ins)


def joined(parts):
    rows = sum(part.shape[0] for part in parts)
    (whole,) = call(join_kernel, [((rows, HEAD_SIZE), bf16)], parts, smem=0)
    return whole


def summed_along_z(own, *parts):
    for r, part in enumerate(parts):
        own = own + z_with(part, r + 1).astype(f32)
    return own


def local(
    hidden_in,
    queries,
    rotary_key_rows,
    value_projection,
    output_gradient,
    attended,
    doc_ids,
    block_place,
):
    dp = lax.axis_index("dp")
    ctx = lax.axis_index("ctx")
    x_hi, core = dp // 2, dp % 2
    x_lo, z = ctx // 4, ctx % 4
    x = x_hi * 2 + x_lo
    rows = queries.shape[1]
    grad_scale = float(rows * 32) ** (-0.5)
    query, grad, saved = queries[0], output_gradient[0], attended[0]
    docs = doc_ids[0].reshape(16, BLOCK)

    def places_of_keys(placing):
        stored = jnp.arange(16, dtype=jnp.int32)
        owner = stored // 2
        lies = ((owner % 4) ^ z) * 4 + ((owner // 4) ^ x_lo) * 2 + stored % 2
        by_place = jnp.sum(jnp.where(placing[None, :] == stored[:, None], lies[None, :], 0), axis=1)
        mine = jnp.sum(
            jnp.where(stored[None, :] == (2 * ctx + jnp.arange(2))[:, None], placing[None, :], 0), axis=1
        )
        return jnp.concatenate([by_place, mine])

    def places_of_slabs(head):
        outer, inner = jnp.arange(16, dtype=jnp.int32) // 4, jnp.arange(16, dtype=jnp.int32) % 4

        def slabs_of(core):
            at_x = x ^ jnp.where(core == 0, outer, inner)
            at_z = z ^ jnp.where(core == 0, inner, outer)
            return (2 * (at_x // 2) + core) * 8 + (at_x % 2) * 4 + at_z

        asked = jnp.stack([head] + [2 * (head ^ d) + core for d in (1, 2, 3)] + [core])
        return jnp.concatenate([slabs_of(core), slabs_of(1 - core), asked]).astype(jnp.int32)

    hidden = hidden_in[0]
    window = ((SPAN, HEAD_SIZE), bf16)
    whole = ((2048, HEAD_SIZE), bf16)
    bias = ((SPAN, BLOCK), f32)
    square = ((SPAN, 1536), bf16)
    stack = ((1536, HEAD_SIZE), bf16)
    sums = [((SPAN, HEAD_SIZE), f32), ((2048, HEAD_SIZE), f32)]
    parts_out = [((512, HEAD_SIZE), f32)] + [((512, HEAD_SIZE), bf16)] * 3
    together = lax.optimization_barrier

    own_keys = rotary_key_rows[0]
    near, first, placing, head = together(
        (
            [own_keys, x_swap(own_keys)],
            [value_projection] + [first_with(value_projection, r) for r in (1, 2, 3)],
            block_place[0],
            lax.axis_index("head"),
        )
    )
    near, first = joined(near), joined(first)

    keys, w1, w3, first, table, slabs = together(
        (
            [near] + [z_with(near, r) for r in (1, 2, 3)],
            second_with(first, 1),
            second_with(first, 3),
            first,
            places_of_keys(placing),
            places_of_slabs(head),
        )
    )

    w2 = second_with(first, 2)
    s0, s1, s3 = core_swap(first), core_swap(w1), core_swap(w3)
    totals, *value_parts = call(
        value_side_kernel,
        [((24, 128), f32)] + parts_out,
        [table, docs, query, grad, *keys],
        scratch=[whole, window, bias, ((SPAN, 256), f32), square, stack] + sums,
        cost=7, limit=24,
    )
    w2, s0, s1, s3, totals, value_parts, slabs = together((w2, s0, s1, s3, totals, value_parts, slabs))

    s2 = core_swap(w2)
    own_values, own_rows, *halves = call(
        project_kernel,
        [((rows, HEAD_SIZE), bf16), ((QUARTER, HEAD_SIZE), bf16)] + [((HALF, HEAD_SIZE), bf16)] * 3,
        [slabs, hidden, first, w1, w2, w3, s0, s1, s2, s3],
        scratch=[((4 * QUARTER, HEAD_SIZE), bf16)],
        cost=4, limit=24,
    )
    arrived = [z_with(part, r + 1) for r, part in enumerate(value_parts[1:])]
    own_values, arrived, value_sum, saved = together((own_values, arrived, value_parts[0], saved))
    for part in arrived:
        value_sum = value_sum + part.astype(f32)

    (terms,) = call(row_terms_kernel, [((24, 128), f32)], [grad, saved], smem=0)
    value_rest = x_swap(value_sum[rows:].astype(bf16))
    near_values, value_rest, value_sum, terms = together(
        ([own_values, x_swap(own_values)], value_rest, value_sum, terms)
    )
    near_values = joined(near_values)
    value_grads = (value_sum[:rows] + value_rest.astype(f32)).astype(bf16)

    message = ((HALF + rows, HEAD_SIZE), bf16)
    w_own, w_other, *messages = call(
        weight_kernel,
        [((2048, SLAB), f32), ((2048, SLAB), bf16)] + [message] * 3,
        [slabs, hidden, value_grads, *halves],
        cost=4, limit=24,
    )
    w_other = core_swap(w_other)
    w_parts = [
        w_own[512 * r : 512 * (r + 1)] + w_other[512 * r : 512 * (r + 1)].astype(f32) for r in range(4)
    ]
    w_parts = [w_parts[0]] + [part.astype(bf16) for part in w_parts[1:]]
    values, w_parts, messages = together(
        ([near_values] + [z_with(near_values, r) for r in (1, 2, 3)], w_parts, messages)
    )

    messages[0], messages[2] = y_with(messages[0], 1), y_with(messages[2], 3)
    w_sum = w_parts[0]
    for r in (1, 2, 3):
        w_sum = w_sum + second_with(w_parts[r], r).astype(f32)
    dquery, *key_parts = call(
        key_side_kernel,
        [((rows, 1536), bf16)] + parts_out,
        [table, docs, query, grad, totals, terms, *keys, *values],
        scratch=[whole, whole, window, window, bias, square, stack] + sums,
        cost=9, limit=28,
    )
    key_parts, w_sum, messages = together((key_parts, w_sum, messages))

    messages[1] = y_with(messages[1], 2)
    swapped = [core_swap(messages[0]), None, core_swap(messages[2])]
    got = [
        first_with(w_sum[i * HEAD_SIZE : (i + 1) * HEAD_SIZE].astype(bf16), i) for i in (1, 2, 3)
    ]
    arrived = [z_with(part, r + 1) for r, part in enumerate(key_parts[1:])]
    arrived, key_sum, messages, swapped[0], swapped[2] = together(
        (arrived, key_parts[0], messages, swapped[0], swapped[2])
    )
    for part in arrived:
        key_sum = key_sum + part.astype(f32)

    swapped[1] = core_swap(messages[1])
    key_grads = (key_sum[:rows] + x_swap(key_sum[rows:].astype(bf16)).astype(f32)).astype(bf16)
    (input_grad,) = call(
        input_kernel,
        [((rows, QUARTER), bf16)],
        [slabs, value_grads, own_rows, *messages, *swapped],
        scratch=[((QUARTER, 512), bf16), ((rows, 512), bf16), pltpu.SemaphoreType.DMA((10,))],
        anys=tuple(range(2, 9)),
        cost=4, limit=16,
    )
    (weight_grad,) = call(
        functools.partial(fold_kernel, grad_scale),
        [((SLAB, HEAD_SIZE), f32)],
        [w_sum[:HEAD_SIZE], *got],
        smem=0,
    )
    return dquery[None], key_grads[None], input_grad[None], weight_grad


def solution(mesh):
    in_specs = (
        P("dp", "ctx", None),
        P("dp", "ctx", "head"),
        P("dp", "ctx", "head"),
        P(("dp", "ctx"), "head"),
        P("dp", "ctx", "head"),
        P("dp", "ctx", "head"),
        P("dp", None),
        P("dp", None),
    )
    out_specs = (
        P("dp", "ctx", "head"),
        P("dp", "ctx", "head"),
        P("dp", "ctx", "head"),
        P(("dp", "ctx"), "head"),
    )
    return jax.shard_map(local, mesh=mesh, in_specs=in_specs, out_specs=out_specs, check_vma=False)
```

```python
import functools

import jax
import jax.numpy as jnp
from jax import lax
from jax.experimental import pallas as pl
from jax.experimental.pallas import tpu as pltpu
from jax.sharding import PartitionSpec as P

HEAD_SIZE = 128
QUERY_PER_KEY = 12
PAIRS = QUERY_PER_KEY // 2
BLOCK = 128
WINDOW = 9
SPAN = WINDOW * BLOCK
SLAB = 384
QUARTER = 3072
HALF = QUARTER // 2
COST_UNIT = 3 << 20
MASKED = -1e30
LOG2E = 1.4426950408889634
SCALING = float(HEAD_SIZE) ** (-0.5)
f32 = jnp.float32
bf16 = jnp.bfloat16


def place_of(index):
    dp, ctx = divmod(index, 8)
    x_hi, core = divmod(dp, 2)
    x_lo, z = divmod(ctx, 4)
    return x_hi * 2 + x_lo, z, core


def index_of(x, z, core):
    x_hi, x_lo = divmod(x % 4, 2)
    return (x_hi * 2 + core) * 8 + x_lo * 4 + z % 4


def moved(value, where):
    pairs = [(i, index_of(*where(*place_of(i)))) for i in range(32)]
    return lax.ppermute(value, ("dp", "ctx"), pairs)


def core_swap(value):
    return moved(value, lambda x, z, c: (x, z, 1 - c))


def x_swap(value):
    return moved(value, lambda x, z, c: (x ^ 1, z, c))


def z_with(value, bits):
    return moved(value, lambda x, z, c: (x, z ^ bits, c))


def first_with(value, bits):
    return moved(value, lambda x, z, c: (x, z ^ bits, c) if c == 0 else (x ^ bits, z, c))


def second_with(value, bits):
    return moved(value, lambda x, z, c: (x ^ bits, z, c) if c == 0 else (x, z ^ bits, c))


def y_with(value, bits):
    return lax.ppermute(value, "head", [(y, y ^ bits) for y in range(4)])


def nt(a, b):
    return lax.dot_general(a, b, (((1,), (1,)), ((), ())), preferred_element_type=f32)


def nn(a, b):
    return lax.dot_general(a, b, (((1,), (0,)), ((), ())), preferred_element_type=f32)


def tn(a, b):
    return lax.dot_general(a, b, (((0,), (0,)), ((), ())), preferred_element_type=f32)


def row_terms_kernel(grad_ref, saved_ref, out_ref):
    for a in range(2):
        rows = slice(a * BLOCK, (a + 1) * BLOCK)
        for h in range(QUERY_PER_KEY):
            cols = slice(h * HEAD_SIZE, (h + 1) * HEAD_SIZE)
            product = grad_ref[rows, cols].astype(f32) * saved_ref[rows, cols].astype(f32)
            at = a * QUERY_PER_KEY + h
            out_ref[at : at + 1, :] = jnp.sum(product.T, axis=0, keepdims=True)


def join_kernel(own, *refs):
    parts, out, sem = refs[:-2], refs[-2], refs[-1]
    rows = parts[0].shape[0]
    copy = pltpu.make_async_copy(own, out.at[:rows, :], sem)
    copy.start()
    for i, part in enumerate(parts):
        out[(i + 1) * rows : (i + 2) * rows, :] = part[...]
    copy.wait()


def fold_kernel(scale, own, one, two, three, out):
    total = own[...] + one[...].astype(f32) + two[...].astype(f32) + three[...].astype(f32)
    out[...] = (total * scale).T


def fill_bias(place, doc_ref, bias_ref):
    docs = doc_ref[...]
    own = doc_ref[pl.ds(place, 1), :]
    start = jnp.zeros((1, BLOCK), f32)
    for d in range(1, 6):
        held = jnp.sum(jnp.where(docs == d - 1, 1.0, 0.0), axis=(0, 1), keepdims=True)
        start = start + jnp.where(own >= d, held, 0.0)
    start = start.astype(jnp.int32)
    query = place * BLOCK + lax.broadcasted_iota(jnp.int32, (1, BLOCK), 1)
    key = (place - (WINDOW - 1)) * BLOCK + lax.broadcasted_iota(jnp.int32, (SPAN, 1), 0)
    bias_ref[...] = jnp.where((key >= start) & (key <= query), 0.0, MASKED)


def fill_window(table_ref, place, parts, win_ref):
    for j in range(WINDOW):
        block = table_ref[jnp.maximum(place - (WINDOW - 1) + j, 0)]
        win_ref[j * BLOCK : (j + 1) * BLOCK, :] = parts[pl.ds(pl.multiple_of(block * BLOCK, BLOCK), BLOCK), :]


def join(parts, all_ref):
    rows = parts[0].shape[0]
    for i, part in enumerate(parts):
        all_ref[i * rows : (i + 1) * rows, :] = part[...]


def stacked(ref, a, pair):
    rows = slice(a * BLOCK, (a + 1) * BLOCK)
    one = ref[rows, pair * 256 : pair * 256 + 128]
    two = ref[rows, pair * 256 + 128 : pair * 256 + 256]
    return jnp.concatenate([one, two], axis=0)


def beside(ref, a, pair):
    at = a * QUERY_PER_KEY + 2 * pair
    return jnp.concatenate([ref[at : at + 1, :], ref[at + 1 : at + 2, :]], axis=1)


def add_window(table_ref, place, win_ref, sum_ref):
    for j in range(WINDOW):
        block = table_ref[jnp.maximum(place - (WINDOW - 1) + j, 0)]
        at = pl.ds(pl.multiple_of(block * BLOCK, BLOCK), BLOCK)
        sum_ref[at, :] += win_ref[j * BLOCK : (j + 1) * BLOCK, :]


def value_side_kernel(
    table_ref, doc_ref, q_ref, g_ref, k0, k1, k2, k3,
    total_ref, o0, o1, o2, o3,
    all_ref, win_ref, bias_ref, score_ref, raised_ref, scaled_ref, acc_ref, sum_ref,
):
    join((k0, k1, k2, k3), all_ref)
    sum_ref[...] = jnp.zeros_like(sum_ref)
    for a in range(2):
        place = table_ref[16 + a]
        fill_bias(place, doc_ref, bias_ref)
        fill_window(table_ref, place, all_ref, win_ref)
        for pair in range(PAIRS):
            cols = slice(pair * 256, (pair + 1) * 256)
            products = nt(win_ref[...], stacked(q_ref, a, pair))
            highest = None
            for j in range(WINDOW):
                keys = slice(j * BLOCK, (j + 1) * BLOCK)
                bias = jnp.concatenate([bias_ref[keys, :]] * 2, axis=1)
                scores = products[keys] * (SCALING * LOG2E) + bias
                score_ref[keys, :] = scores
                highest = scores if highest is None else jnp.maximum(highest, scores)
            highest = jnp.max(highest, axis=0, keepdims=True)
            total = None
            for j in range(WINDOW):
                keys = slice(j * BLOCK, (j + 1) * BLOCK)
                raised = jnp.exp2(score_ref[keys, :] - highest)
                total = raised if total is None else total + raised
                raised_ref[keys, cols] = raised.astype(bf16)
            total = jnp.sum(total, axis=0, keepdims=True)
            log_total = highest + jnp.log2(total)
            share = 1.0 / total
            for half in range(2):
                h = 2 * pair + half
                lanes = slice(half * BLOCK, (half + 1) * BLOCK)
                at = a * QUERY_PER_KEY + h
                total_ref[at : at + 1, :] = log_total[:, lanes]
                factor = jnp.broadcast_to(share[:, lanes], (BLOCK, BLOCK)).T
                grads = g_ref[a * BLOCK : (a + 1) * BLOCK, h * HEAD_SIZE : (h + 1) * HEAD_SIZE]
                scaled_ref[h * BLOCK : (h + 1) * BLOCK, :] = (grads.astype(f32) * factor).astype(bf16)
        acc_ref[...] = nn(raised_ref[...], scaled_ref[...])
        add_window(table_ref, place, acc_ref, sum_ref)
    o0[...] = sum_ref[0:512, :]
    for i, out in enumerate((o1, o2, o3)):
        out[...] = sum_ref[512 * (i + 1) : 512 * (i + 2), :].astype(bf16)


def key_side_kernel(
    table_ref, doc_ref, q_ref, g_ref, total_ref, term_ref, k0, k1, k2, k3, v0, v1, v2, v3,
    dq_ref, o0, o1, o2, o3,
    allk_ref, allv_ref, wink_ref, winv_ref, bias_ref, ds_ref, qs_ref, acc_ref, sum_ref,
):
    join((k0, k1, k2, k3), allk_ref)
    join((v0, v1, v2, v3), allv_ref)
    sum_ref[...] = jnp.zeros_like(sum_ref)
    for a in range(2):
        place = table_ref[16 + a]
        fill_bias(place, doc_ref, bias_ref)
        fill_window(table_ref, place, allk_ref, wink_ref)
        fill_window(table_ref, place, allv_ref, winv_ref)
        for pair in range(PAIRS):
            cols = slice(pair * 256, (pair + 1) * 256)
            query = stacked(q_ref, a, pair)
            qs_ref[cols, :] = query
            products = nt(wink_ref[...], query)
            dprobs = nt(winv_ref[...], stacked(g_ref, a, pair))
            log_total = beside(total_ref, a, pair)
            terms = beside(term_ref, a, pair)
            for j in range(WINDOW):
                keys = slice(j * BLOCK, (j + 1) * BLOCK)
                bias = jnp.concatenate([bias_ref[keys, :]] * 2, axis=1)
                probs = jnp.exp2(products[keys] * (SCALING * LOG2E) + bias - log_total)
                ds_ref[keys, cols] = (probs * (dprobs[keys] - terms)).astype(bf16)
        dquery = tn(wink_ref[...], ds_ref[...]) * SCALING
        for h in range(QUERY_PER_KEY):
            dq_ref[a * BLOCK : (a + 1) * BLOCK, h * HEAD_SIZE : (h + 1) * HEAD_SIZE] = (
                dquery[:, h * BLOCK : (h + 1) * BLOCK].T.astype(bf16)
            )
        acc_ref[...] = nn(ds_ref[...], qs_ref[...])
        add_window(table_ref, place, acc_ref, sum_ref)
    o0[...] = sum_ref[0:512, :] * SCALING
    for i, out in enumerate((o1, o2, o3)):
        out[...] = (sum_ref[512 * (i + 1) : 512 * (i + 2), :] * SCALING).astype(bf16)


def project_kernel(
    table_ref, hidden, w0, w1, w2, w3, s0, s1, s2, s3, out, own_rows, r1, r2, r3, all_ref
):
    for k, w in enumerate((w0, w1, w2, w3, s0, s1, s2, s3)):
        for i in range(4):
            at = pl.multiple_of(table_ref[k * 4 + i] * SLAB, BLOCK)
            all_ref[pl.ds(at, SLAB), :] = w[i * SLAB : (i + 1) * SLAB, :]
    out[...] = nn(hidden[...], all_ref[...]).astype(bf16)
    own_rows[...] = all_ref[pl.ds(pl.multiple_of(table_ref[32] * QUARTER, BLOCK), QUARTER), :]
    for d, r in enumerate((r1, r2, r3)):
        r[...] = all_ref[pl.ds(pl.multiple_of(table_ref[33 + d] * HALF, BLOCK), HALF), :]


def weight_kernel(table_ref, hidden, grads, r1, r2, r3, own, other, m1, m2, m3):
    turned = grads[...].T
    for k in range(16):
        for out, at in ((other, 16 + k), (own, k)):
            cols = pl.ds(pl.multiple_of(table_ref[at] * SLAB, BLOCK), SLAB)
            block = nn(turned, hidden[:, cols])
            out[k * HEAD_SIZE : (k + 1) * HEAD_SIZE, :] = block.astype(out.dtype)
    for r, m in ((r1, m1), (r2, m2), (r3, m3)):
        m[:HALF, :] = r[...]
        m[HALF:, :] = grads[...]


def input_kernel(table_ref, grads, own, a1, a2, a3, b1, b2, b3, out, rows_ref, grads_ref, sems):
    mine = pl.multiple_of(table_ref[36] * HALF, BLOCK)
    other = pl.multiple_of((1 - table_ref[36]) * HALF, BLOCK)
    copies = [pltpu.make_async_copy(own, rows_ref.at[:, 0:BLOCK], sems.at[0])]
    for d, (a, b) in enumerate(((a1, b1), (a2, b2), (a3, b3))):
        cols = slice((d + 1) * BLOCK, (d + 2) * BLOCK)
        pieces = (
            (a.at[0:HALF, :], rows_ref.at[pl.ds(mine, HALF), cols]),
            (b.at[0:HALF, :], rows_ref.at[pl.ds(other, HALF), cols]),
            (a.at[HALF : HALF + 256, :], grads_ref.at[:, cols]),
        )
        for i, (source, target) in enumerate(pieces):
            copies.append(pltpu.make_async_copy(source, target, sems.at[3 * d + 1 + i]))
    for copy in copies:
        copy.start()
    grads_ref[:, 0:BLOCK] = grads[...]
    for copy in copies:
        copy.wait()
    for part in range(4):
        cols = slice(part * 768, (part + 1) * 768)
        out[:, cols] = nt(grads_ref[...], rows_ref[cols, :]).astype(bf16)


SMEM = pl.BlockSpec(memory_space=pltpu.SMEM)
VMEM = pl.BlockSpec(memory_space=pltpu.VMEM)


def call(kernel, outs, ins, scratch=(), cost=1, smem=1, anys=(), limit=8):
    any_spec = pl.BlockSpec(memory_space=pl.ANY)
    specs = [SMEM] * smem + [any_spec if i in anys else VMEM for i in range(smem, len(ins))]
    return pl.pallas_call(
        kernel,
        out_shape=tuple(jax.ShapeDtypeStruct(s, d) for s, d in outs),
        in_specs=specs,
        out_specs=tuple(VMEM for _ in outs),
        scratch_shapes=[s if not isinstance(s, tuple) else pltpu.VMEM(*s) for s in scratch],
        compiler_params=pltpu.CompilerParams(vmem_limit_bytes=limit * 1024 * 1024),
        cost_estimate=pl.CostEstimate(
            flops=0, bytes_accessed=int(cost * COST_UNIT), transcendentals=0
        ),
    )(*ins)


def joined(parts):
    rows = sum(part.shape[0] for part in parts)
    (whole,) = call(
        join_kernel,
        [((rows, HEAD_SIZE), bf16)],
        parts,
        scratch=[pltpu.SemaphoreType.DMA],
        smem=0, anys=(0,),
    )
    return whole


def summed_along_z(own, *parts):
    for r, part in enumerate(parts):
        own = own + z_with(part, r + 1).astype(f32)
    return own


def local(
    hidden_in,
    queries,
    rotary_key_rows,
    value_projection,
    output_gradient,
    attended,
    doc_ids,
    block_place,
):
    dp = lax.axis_index("dp")
    ctx = lax.axis_index("ctx")
    x_hi, core = dp // 2, dp % 2
    x_lo, z = ctx // 4, ctx % 4
    x = x_hi * 2 + x_lo
    rows = queries.shape[1]
    grad_scale = float(rows * 32) ** (-0.5)
    query, grad, saved = queries[0], output_gradient[0], attended[0]
    docs = doc_ids[0].reshape(16, BLOCK)

    def places_of_keys(placing):
        stored = jnp.arange(16, dtype=jnp.int32)
        owner = stored // 2
        lies = ((owner % 4) ^ z) * 4 + ((owner // 4) ^ x_lo) * 2 + stored % 2
        by_place = jnp.sum(jnp.where(placing[None, :] == stored[:, None], lies[None, :], 0), axis=1)
        mine = jnp.sum(
            jnp.where(stored[None, :] == (2 * ctx + jnp.arange(2))[:, None], placing[None, :], 0), axis=1
        )
        return jnp.concatenate([by_place, mine])

    def places_of_slabs(head):
        outer, inner = jnp.arange(16, dtype=jnp.int32) // 4, jnp.arange(16, dtype=jnp.int32) % 4

        def slabs_of(core):
            at_x = x ^ jnp.where(core == 0, outer, inner)
            at_z = z ^ jnp.where(core == 0, inner, outer)
            return (2 * (at_x // 2) + core) * 8 + (at_x % 2) * 4 + at_z

        asked = jnp.stack([head] + [2 * (head ^ d) + core for d in (1, 2, 3)] + [core])
        return jnp.concatenate([slabs_of(core), slabs_of(1 - core), asked]).astype(jnp.int32)

    hidden = hidden_in[0]
    window = ((SPAN, HEAD_SIZE), bf16)
    whole = ((2048, HEAD_SIZE), bf16)
    bias = ((SPAN, BLOCK), f32)
    square = ((SPAN, 1536), bf16)
    stack = ((1536, HEAD_SIZE), bf16)
    sums = [((SPAN, HEAD_SIZE), f32), ((2048, HEAD_SIZE), f32)]
    parts_out = [((512, HEAD_SIZE), f32)] + [((512, HEAD_SIZE), bf16)] * 3
    together = lax.optimization_barrier

    own_keys = rotary_key_rows[0]
    near, first, placing, head = together(
        (
            [own_keys, x_swap(own_keys)],
            [value_projection] + [first_with(value_projection, r) for r in (1, 2, 3)],
            block_place[0],
            lax.axis_index("head"),
        )
    )
    near, first = joined(near), joined(first)

    keys, w1, w3, first, table, slabs = together(
        (
            [near] + [z_with(near, r) for r in (1, 2, 3)],
            second_with(first, 1),
            second_with(first, 3),
            first,
            places_of_keys(placing),
            places_of_slabs(head),
        )
    )

    w2 = second_with(w3, 1)
    s0, s1, s3 = core_swap(first), core_swap(w1), core_swap(w3)
    totals, *value_parts = call(
        value_side_kernel,
        [((24, 128), f32)] + parts_out,
        [table, docs, query, grad, *keys],
        scratch=[whole, window, bias, ((SPAN, 256), f32), square, stack] + sums,
        cost=7, limit=24,
    )
    w2, s0, s1, s3, totals, value_parts, slabs = together((w2, s0, s1, s3, totals, value_parts, slabs))

    s2 = core_swap(w2)
    own_values, own_rows, *halves = call(
        project_kernel,
        [((rows, HEAD_SIZE), bf16), ((QUARTER, HEAD_SIZE), bf16)] + [((HALF, HEAD_SIZE), bf16)] * 3,
        [slabs, hidden, first, w1, w2, w3, s0, s1, s2, s3],
        scratch=[((4 * QUARTER, HEAD_SIZE), bf16)],
        cost=4, limit=24,
    )
    arrived = [z_with(part, r + 1) for r, part in enumerate(value_parts[1:])]
    own_values, arrived, value_sum, saved = together((own_values, arrived, value_parts[0], saved))
    for part in arrived:
        value_sum = value_sum + part.astype(f32)

    (terms,) = call(row_terms_kernel, [((24, 128), f32)], [grad, saved], smem=0)
    value_rest = x_swap(value_sum[rows:].astype(bf16))
    near_values, value_rest, value_sum, terms = together(
        ([own_values, x_swap(own_values)], value_rest, value_sum, terms)
    )
    near_values = joined(near_values)
    value_grads = (value_sum[:rows] + value_rest.astype(f32)).astype(bf16)

    message = ((HALF + rows, HEAD_SIZE), bf16)
    w_own, w_other, *messages = call(
        weight_kernel,
        [((2048, SLAB), f32), ((2048, SLAB), bf16)] + [message] * 3,
        [slabs, hidden, value_grads, *halves],
        cost=4, limit=24,
    )
    w_other = core_swap(w_other)
    w_parts = [
        w_own[512 * r : 512 * (r + 1)] + w_other[512 * r : 512 * (r + 1)].astype(f32) for r in range(4)
    ]
    w_parts = [w_parts[0]] + [part.astype(bf16) for part in w_parts[1:]]
    messages[0], messages[2] = y_with(messages[0], 1), y_with(messages[2], 3)
    values, w_parts, messages = together(
        ([near_values] + [z_with(near_values, r) for r in (1, 2, 3)], w_parts, messages)
    )

    messages[1] = y_with(messages[1], 2)
    swapped = [core_swap(messages[0]), None, core_swap(messages[2])]
    w_sum = w_parts[0]
    for r in (1, 2, 3):
        w_sum = w_sum + second_with(w_parts[r], r).astype(f32)
    dquery, *key_parts = call(
        key_side_kernel,
        [((rows, 1536), bf16)] + parts_out,
        [table, docs, query, grad, totals, terms, *keys, *values],
        scratch=[whole, whole, window, window, bias, square, stack] + sums,
        cost=9, limit=28,
    )
    key_parts, w_sum, messages, swapped[0], swapped[2] = together(
        (key_parts, w_sum, messages, swapped[0], swapped[2])
    )

    swapped[1] = core_swap(messages[1])
    got = [
        first_with(w_sum[i * HEAD_SIZE : (i + 1) * HEAD_SIZE].astype(bf16), i) for i in (1, 2, 3)
    ]
    arrived = [z_with(part, r + 1) for r, part in enumerate(key_parts[1:])]
    arrived, key_sum, slabs, swapped[1] = together((arrived, key_parts[0], slabs, swapped[1]))
    for part in arrived:
        key_sum = key_sum + part.astype(f32)

    key_grads = (key_sum[:rows] + x_swap(key_sum[rows:].astype(bf16)).astype(f32)).astype(bf16)
    (input_grad,) = call(
        input_kernel,
        [((rows, QUARTER), bf16)],
        [slabs, value_grads, own_rows, *messages, *swapped],
        scratch=[((QUARTER, 512), bf16), ((rows, 512), bf16), pltpu.SemaphoreType.DMA((10,))],
        anys=tuple(range(2, 9)),
        cost=4, limit=16,
    )
    got, input_grad = together((got, input_grad))
    (weight_grad,) = call(
        functools.partial(fold_kernel, grad_scale),
        [((SLAB, HEAD_SIZE), f32)],
        [w_sum[:HEAD_SIZE], *got],
        smem=0,
    )
    return dquery[None], key_grads[None], input_grad[None], weight_grad


def solution(mesh):
    in_specs = (
        P("dp", "ctx", None),
        P("dp", "ctx", "head"),
        P("dp", "ctx", "head"),
        P(("dp", "ctx"), "head"),
        P("dp", "ctx", "head"),
        P("dp", "ctx", "head"),
        P("dp", None),
        P("dp", None),
    )
    out_specs = (
        P("dp", "ctx", "head"),
        P("dp", "ctx", "head"),
        P("dp", "ctx", "head"),
        P(("dp", "ctx"), "head"),
    )
    return jax.shard_map(local, mesh=mesh, in_specs=in_specs, out_specs=out_specs, check_vma=False)
```

```python
import functools

import jax
import jax.numpy as jnp
from jax import lax
from jax.experimental import pallas as pl
from jax.experimental.pallas import tpu as pltpu
from jax.sharding import PartitionSpec as P

HEAD_SIZE = 128
QUERY_PER_KEY = 12
PAIRS = QUERY_PER_KEY // 2
BLOCK = 128
WINDOW = 9
SPAN = WINDOW * BLOCK
SLAB = 384
QUARTER = 3072
HALF = QUARTER // 2
COST_UNIT = 3 << 20
MASKED = -1e30
LOG2E = 1.4426950408889634
SCALING = float(HEAD_SIZE) ** (-0.5)
f32 = jnp.float32
bf16 = jnp.bfloat16


def place_of(index):
    dp, ctx = divmod(index, 8)
    x_hi, core = divmod(dp, 2)
    x_lo, z = divmod(ctx, 4)
    return x_hi * 2 + x_lo, z, core


def index_of(x, z, core):
    x_hi, x_lo = divmod(x % 4, 2)
    return (x_hi * 2 + core) * 8 + x_lo * 4 + z % 4


def moved(value, where):
    pairs = [(i, index_of(*where(*place_of(i)))) for i in range(32)]
    return lax.ppermute(value, ("dp", "ctx"), pairs)


def core_swap(value):
    return moved(value, lambda x, z, c: (x, z, 1 - c))


def x_swap(value):
    return moved(value, lambda x, z, c: (x ^ 1, z, c))


def z_with(value, bits):
    return moved(value, lambda x, z, c: (x, z ^ bits, c))


def first_with(value, bits):
    return moved(value, lambda x, z, c: (x, z ^ bits, c) if c == 0 else (x ^ bits, z, c))


def second_with(value, bits):
    return moved(value, lambda x, z, c: (x ^ bits, z, c) if c == 0 else (x, z ^ bits, c))


def y_with(value, bits):
    return lax.ppermute(value, "head", [(y, y ^ bits) for y in range(4)])


def nt(a, b):
    return lax.dot_general(a, b, (((1,), (1,)), ((), ())), preferred_element_type=f32)


def nn(a, b):
    return lax.dot_general(a, b, (((1,), (0,)), ((), ())), preferred_element_type=f32)


def tn(a, b):
    return lax.dot_general(a, b, (((0,), (0,)), ((), ())), preferred_element_type=f32)


def row_terms_kernel(grad_ref, saved_ref, out_ref):
    for a in range(2):
        rows = slice(a * BLOCK, (a + 1) * BLOCK)
        for h in range(QUERY_PER_KEY):
            cols = slice(h * HEAD_SIZE, (h + 1) * HEAD_SIZE)
            product = grad_ref[rows, cols].astype(f32) * saved_ref[rows, cols].astype(f32)
            at = a * QUERY_PER_KEY + h
            out_ref[at : at + 1, :] = jnp.sum(product.T, axis=0, keepdims=True)


def join_kernel(own, *refs):
    parts, out, sem = refs[:-2], refs[-2], refs[-1]
    rows = parts[0].shape[0]
    copy = pltpu.make_async_copy(own, out.at[:rows, :], sem)
    copy.start()
    for i, part in enumerate(parts):
        out[(i + 1) * rows : (i + 2) * rows, :] = part[...]
    copy.wait()


def fold_kernel(scale, own, one, two, three, out):
    total = own[...] + one[...].astype(f32) + two[...].astype(f32) + three[...].astype(f32)
    out[...] = (total * scale).T


def fill_bias(place, doc_ref, bias_ref):
    docs = doc_ref[...]
    own = doc_ref[pl.ds(place, 1), :]
    start = jnp.zeros((1, BLOCK), f32)
    for d in range(1, 6):
        held = jnp.sum(jnp.where(docs == d - 1, 1.0, 0.0), axis=(0, 1), keepdims=True)
        start = start + jnp.where(own >= d, held, 0.0)
    start = start.astype(jnp.int32)
    query = place * BLOCK + lax.broadcasted_iota(jnp.int32, (1, BLOCK), 1)
    key = (place - (WINDOW - 1)) * BLOCK + lax.broadcasted_iota(jnp.int32, (SPAN, 1), 0)
    bias_ref[...] = jnp.where((key >= start) & (key <= query), 0.0, MASKED)


def fill_window(table_ref, place, parts, win_ref):
    for j in range(WINDOW):
        block = table_ref[jnp.maximum(place - (WINDOW - 1) + j, 0)]
        win_ref[j * BLOCK : (j + 1) * BLOCK, :] = parts[pl.ds(pl.multiple_of(block * BLOCK, BLOCK), BLOCK), :]


def join(parts, all_ref):
    rows = parts[0].shape[0]
    for i, part in enumerate(parts):
        all_ref[i * rows : (i + 1) * rows, :] = part[...]


def stacked(ref, a, pair):
    rows = slice(a * BLOCK, (a + 1) * BLOCK)
    one = ref[rows, pair * 256 : pair * 256 + 128]
    two = ref[rows, pair * 256 + 128 : pair * 256 + 256]
    return jnp.concatenate([one, two], axis=0)


def beside(ref, a, pair):
    at = a * QUERY_PER_KEY + 2 * pair
    return jnp.concatenate([ref[at : at + 1, :], ref[at + 1 : at + 2, :]], axis=1)


def add_window(table_ref, place, win_ref, sum_ref):
    for j in range(WINDOW):
        block = table_ref[jnp.maximum(place - (WINDOW - 1) + j, 0)]
        at = pl.ds(pl.multiple_of(block * BLOCK, BLOCK), BLOCK)
        sum_ref[at, :] += win_ref[j * BLOCK : (j + 1) * BLOCK, :]


def value_side_kernel(
    table_ref, doc_ref, q_any, g_any, k0, k1, k2, k3,
    total_ref, o0, o1, o2, o3,
    q_ref, g_ref, all_ref, win_ref, bias_ref, score_ref, raised_ref, scaled_ref, acc_ref, sum_ref, sems,
):
    copies = [
        pltpu.make_async_copy(q_any, q_ref, sems.at[0]),
        pltpu.make_async_copy(g_any, g_ref, sems.at[1]),
    ]
    for copy in copies:
        copy.start()
    join((k0, k1, k2, k3), all_ref)
    sum_ref[...] = jnp.zeros_like(sum_ref)
    for a in range(2):
        place = table_ref[16 + a]
        fill_bias(place, doc_ref, bias_ref)
        fill_window(table_ref, place, all_ref, win_ref)
        if a == 0:
            for copy in copies:
                copy.wait()
        for pair in range(PAIRS):
            cols = slice(pair * 256, (pair + 1) * 256)
            products = nt(win_ref[...], stacked(q_ref, a, pair))
            highest = None
            for j in range(WINDOW):
                keys = slice(j * BLOCK, (j + 1) * BLOCK)
                bias = jnp.concatenate([bias_ref[keys, :]] * 2, axis=1)
                scores = products[keys] * (SCALING * LOG2E) + bias
                score_ref[keys, :] = scores
                highest = scores if highest is None else jnp.maximum(highest, scores)
            highest = jnp.max(highest, axis=0, keepdims=True)
            total = None
            for j in range(WINDOW):
                keys = slice(j * BLOCK, (j + 1) * BLOCK)
                raised = jnp.exp2(score_ref[keys, :] - highest)
                total = raised if total is None else total + raised
                raised_ref[keys, cols] = raised.astype(bf16)
            total = jnp.sum(total, axis=0, keepdims=True)
            log_total = highest + jnp.log2(total)
            share = 1.0 / total
            for half in range(2):
                h = 2 * pair + half
                lanes = slice(half * BLOCK, (half + 1) * BLOCK)
                at = a * QUERY_PER_KEY + h
                total_ref[at : at + 1, :] = log_total[:, lanes]
                factor = jnp.broadcast_to(share[:, lanes], (BLOCK, BLOCK)).T
                grads = g_ref[a * BLOCK : (a + 1) * BLOCK, h * HEAD_SIZE : (h + 1) * HEAD_SIZE]
                scaled_ref[h * BLOCK : (h + 1) * BLOCK, :] = (grads.astype(f32) * factor).astype(bf16)
        acc_ref[...] = nn(raised_ref[...], scaled_ref[...])
        add_window(table_ref, place, acc_ref, sum_ref)
    o0[...] = sum_ref[0:512, :]
    for i, out in enumerate((o1, o2, o3)):
        out[...] = sum_ref[512 * (i + 1) : 512 * (i + 2), :].astype(bf16)


def key_side_kernel(
    table_ref, doc_ref, q_ref, g_ref, total_ref, term_ref, k0, k1, k2, k3, v0, v1, v2, v3,
    dq_ref, o0, o1, o2, o3,
    allk_ref, allv_ref, wink_ref, winv_ref, bias_ref, ds_ref, qs_ref, acc_ref, sum_ref,
):
    join((k0, k1, k2, k3), allk_ref)
    join((v0, v1, v2, v3), allv_ref)
    sum_ref[...] = jnp.zeros_like(sum_ref)
    for a in range(2):
        place = table_ref[16 + a]
        fill_bias(place, doc_ref, bias_ref)
        fill_window(table_ref, place, allk_ref, wink_ref)
        fill_window(table_ref, place, allv_ref, winv_ref)
        for pair in range(PAIRS):
            cols = slice(pair * 256, (pair + 1) * 256)
            query = stacked(q_ref, a, pair)
            qs_ref[cols, :] = query
            products = nt(wink_ref[...], query)
            dprobs = nt(winv_ref[...], stacked(g_ref, a, pair))
            log_total = beside(total_ref, a, pair)
            terms = beside(term_ref, a, pair)
            for j in range(WINDOW):
                keys = slice(j * BLOCK, (j + 1) * BLOCK)
                bias = jnp.concatenate([bias_ref[keys, :]] * 2, axis=1)
                probs = jnp.exp2(products[keys] * (SCALING * LOG2E) + bias - log_total)
                ds_ref[keys, cols] = (probs * (dprobs[keys] - terms)).astype(bf16)
        dquery = tn(wink_ref[...], ds_ref[...]) * SCALING
        for h in range(QUERY_PER_KEY):
            dq_ref[a * BLOCK : (a + 1) * BLOCK, h * HEAD_SIZE : (h + 1) * HEAD_SIZE] = (
                dquery[:, h * BLOCK : (h + 1) * BLOCK].T.astype(bf16)
            )
        acc_ref[...] = nn(ds_ref[...], qs_ref[...])
        add_window(table_ref, place, acc_ref, sum_ref)
    o0[...] = sum_ref[0:512, :] * SCALING
    for i, out in enumerate((o1, o2, o3)):
        out[...] = (sum_ref[512 * (i + 1) : 512 * (i + 2), :] * SCALING).astype(bf16)


def project_kernel(
    table_ref, hidden, w0, w1, w2, w3, s0, s1, s2, s3,
    out, own_rows, r1, r2, r3, hidden_ref, all_ref, sems,
):
    copies = [
        pltpu.make_async_copy(
            hidden.at[:, i * QUARTER : (i + 1) * QUARTER],
            hidden_ref.at[:, i * QUARTER : (i + 1) * QUARTER],
            sems.at[i],
        )
        for i in range(4)
    ]
    for copy in copies:
        copy.start()
    for k, w in enumerate((w0, w1, w2, w3, s0, s1, s2, s3)):
        for i in range(4):
            at = pl.multiple_of(table_ref[k * 4 + i] * SLAB, BLOCK)
            all_ref[pl.ds(at, SLAB), :] = w[i * SLAB : (i + 1) * SLAB, :]
    own_rows[...] = all_ref[pl.ds(pl.multiple_of(table_ref[32] * QUARTER, BLOCK), QUARTER), :]
    for d, r in enumerate((r1, r2, r3)):
        r[...] = all_ref[pl.ds(pl.multiple_of(table_ref[33 + d] * HALF, BLOCK), HALF), :]
    total = jnp.zeros(out.shape, f32)
    for i, copy in enumerate(copies):
        copy.wait()
        part = slice(i * QUARTER, (i + 1) * QUARTER)
        total = total + nn(hidden_ref[:, part], all_ref[part, :])
    out[...] = total.astype(bf16)


def weight_kernel(table_ref, hidden, grads, r1, r2, r3, own, other, m1, m2, m3):
    turned = grads[...].T
    for k in range(16):
        for out, at in ((other, 16 + k), (own, k)):
            cols = pl.ds(pl.multiple_of(table_ref[at] * SLAB, BLOCK), SLAB)
            block = nn(turned, hidden[:, cols])
            out[k * HEAD_SIZE : (k + 1) * HEAD_SIZE, :] = block.astype(out.dtype)
    for r, m in ((r1, m1), (r2, m2), (r3, m3)):
        m[:HALF, :] = r[...]
        m[HALF:, :] = grads[...]


def input_kernel(table_ref, grads, own, a1, a2, a3, b1, b2, b3, out, rows_ref, grads_ref, sems):
    mine = pl.multiple_of(table_ref[36] * HALF, BLOCK)
    other = pl.multiple_of((1 - table_ref[36]) * HALF, BLOCK)
    copies = [pltpu.make_async_copy(own, rows_ref.at[:, 0:BLOCK], sems.at[0])]
    for d, (a, b) in enumerate(((a1, b1), (a2, b2), (a3, b3))):
        cols = slice((d + 1) * BLOCK, (d + 2) * BLOCK)
        pieces = (
            (a.at[0:HALF, :], rows_ref.at[pl.ds(mine, HALF), cols]),
            (b.at[0:HALF, :], rows_ref.at[pl.ds(other, HALF), cols]),
            (a.at[HALF : HALF + 256, :], grads_ref.at[:, cols]),
        )
        for i, (source, target) in enumerate(pieces):
            copies.append(pltpu.make_async_copy(source, target, sems.at[3 * d + 1 + i]))
    for copy in copies:
        copy.start()
    grads_ref[:, 0:BLOCK] = grads[...]
    for copy in copies:
        copy.wait()
    for part in range(4):
        cols = slice(part * 768, (part + 1) * 768)
        out[:, cols] = nt(grads_ref[...], rows_ref[cols, :]).astype(bf16)


SMEM = pl.BlockSpec(memory_space=pltpu.SMEM)
VMEM = pl.BlockSpec(memory_space=pltpu.VMEM)


def call(kernel, outs, ins, scratch=(), cost=1, smem=1, anys=(), limit=8):
    any_spec = pl.BlockSpec(memory_space=pl.ANY)
    specs = [SMEM] * smem + [any_spec if i in anys else VMEM for i in range(smem, len(ins))]
    return pl.pallas_call(
        kernel,
        out_shape=tuple(jax.ShapeDtypeStruct(s, d) for s, d in outs),
        in_specs=specs,
        out_specs=tuple(VMEM for _ in outs),
        scratch_shapes=[s if not isinstance(s, tuple) else pltpu.VMEM(*s) for s in scratch],
        compiler_params=pltpu.CompilerParams(vmem_limit_bytes=limit * 1024 * 1024),
        cost_estimate=pl.CostEstimate(
            flops=0, bytes_accessed=int(cost * COST_UNIT), transcendentals=0
        ),
    )(*ins)


def joined(parts):
    rows = sum(part.shape[0] for part in parts)
    (whole,) = call(
        join_kernel,
        [((rows, HEAD_SIZE), bf16)],
        parts,
        scratch=[pltpu.SemaphoreType.DMA],
        smem=0, anys=(0,),
    )
    return whole


def summed_along_z(own, *parts):
    for r, part in enumerate(parts):
        own = own + z_with(part, r + 1).astype(f32)
    return own


def local(
    hidden_in,
    queries,
    rotary_key_rows,
    value_projection,
    output_gradient,
    attended,
    doc_ids,
    block_place,
):
    dp = lax.axis_index("dp")
    ctx = lax.axis_index("ctx")
    x_hi, core = dp // 2, dp % 2
    x_lo, z = ctx // 4, ctx % 4
    x = x_hi * 2 + x_lo
    rows = queries.shape[1]
    grad_scale = float(rows * 32) ** (-0.5)
    query, grad, saved = queries[0], output_gradient[0], attended[0]

    def places_of_keys(placing):
        stored = jnp.arange(16, dtype=jnp.int32)
        owner = stored // 2
        lies = ((owner % 4) ^ z) * 4 + ((owner // 4) ^ x_lo) * 2 + stored % 2
        by_place = jnp.sum(jnp.where(placing[None, :] == stored[:, None], lies[None, :], 0), axis=1)
        mine = jnp.sum(
            jnp.where(stored[None, :] == (2 * ctx + jnp.arange(2))[:, None], placing[None, :], 0), axis=1
        )
        return jnp.concatenate([by_place, mine])

    def places_of_slabs(head):
        outer, inner = jnp.arange(16, dtype=jnp.int32) // 4, jnp.arange(16, dtype=jnp.int32) % 4

        def slabs_of(core):
            at_x = x ^ jnp.where(core == 0, outer, inner)
            at_z = z ^ jnp.where(core == 0, inner, outer)
            return (2 * (at_x // 2) + core) * 8 + (at_x % 2) * 4 + at_z

        asked = jnp.stack([head] + [2 * (head ^ d) + core for d in (1, 2, 3)] + [core])
        return jnp.concatenate([slabs_of(core), slabs_of(1 - core), asked]).astype(jnp.int32)

    hidden = hidden_in[0]
    window = ((SPAN, HEAD_SIZE), bf16)
    whole = ((2048, HEAD_SIZE), bf16)
    bias = ((SPAN, BLOCK), f32)
    square = ((SPAN, 1536), bf16)
    stack = ((1536, HEAD_SIZE), bf16)
    sums = [((SPAN, HEAD_SIZE), f32), ((2048, HEAD_SIZE), f32)]
    parts_out = [((512, HEAD_SIZE), f32)] + [((512, HEAD_SIZE), bf16)] * 3
    together = lax.optimization_barrier

    own_keys = rotary_key_rows[0]
    near, first, placing, head, docs = together(
        (
            [own_keys, x_swap(own_keys)],
            [value_projection] + [first_with(value_projection, r) for r in (1, 2, 3)],
            block_place[0],
            lax.axis_index("head"),
            jnp.maximum(doc_ids[0], 0).reshape(16, BLOCK),
        )
    )
    near, first = joined(near), joined(first)

    keys, w1, w3, first, table, slabs = together(
        (
            [near] + [z_with(near, r) for r in (1, 2, 3)],
            second_with(first, 1),
            second_with(first, 3),
            first,
            places_of_keys(placing),
            places_of_slabs(head),
        )
    )

    w2 = second_with(w3, 1)
    s0, s1, s3 = core_swap(first), core_swap(w1), core_swap(w3)
    totals, *value_parts = call(
        value_side_kernel,
        [((24, 128), f32)] + parts_out,
        [table, docs, query, grad, *keys],
        scratch=[((rows, 1536), bf16)] * 2
        + [whole, window, bias, ((SPAN, 256), f32), square, stack]
        + sums
        + [pltpu.SemaphoreType.DMA((2,))],
        anys=(2, 3), cost=7, limit=48,
    )
    w2, s0, s1, s3, totals, value_parts, slabs = together((w2, s0, s1, s3, totals, value_parts, slabs))

    s2 = core_swap(w2)
    own_values, own_rows, *halves = call(
        project_kernel,
        [((rows, HEAD_SIZE), bf16), ((QUARTER, HEAD_SIZE), bf16)] + [((HALF, HEAD_SIZE), bf16)] * 3,
        [slabs, hidden, first, w1, w2, w3, s0, s1, s2, s3],
        scratch=[
            ((rows, 4 * QUARTER), bf16),
            ((4 * QUARTER, HEAD_SIZE), bf16),
            pltpu.SemaphoreType.DMA((4,)),
        ],
        anys=(1,), cost=4, limit=48,
    )
    arrived = [z_with(part, r + 1) for r, part in enumerate(value_parts[1:])]
    own_values, halves = together((own_values, halves))

    near_values, value_sum = together(([own_values, x_swap(own_values)], value_parts[0]))
    near_values = joined(near_values)
    for part in arrived:
        value_sum = value_sum + part.astype(f32)
    value_rest = x_swap(value_sum[rows:].astype(bf16))

    values = [near_values] + [z_with(near_values, r) for r in (1, 2, 3)]
    (terms,) = call(row_terms_kernel, [((24, 128), f32)], [grad, saved], smem=0)
    values, value_sum, value_rest, terms = together((values, value_sum, value_rest, terms))
    value_grads = (value_sum[:rows] + value_rest.astype(f32)).astype(bf16)

    message = ((HALF + rows, HEAD_SIZE), bf16)
    w_own, w_other, *messages = call(
        weight_kernel,
        [((2048, SLAB), f32), ((2048, SLAB), bf16)] + [message] * 3,
        [slabs, hidden, value_grads, *halves],
        cost=4, limit=24,
    )
    w_other = core_swap(w_other)
    w_parts = [
        w_own[512 * r : 512 * (r + 1)] + w_other[512 * r : 512 * (r + 1)].astype(f32) for r in range(4)
    ]
    w_parts = [w_parts[0]] + [part.astype(bf16) for part in w_parts[1:]]
    messages[0], messages[2] = y_with(messages[0], 1), y_with(messages[2], 3)
    w_got = [w_parts[0]] + [second_with(w_parts[r], r) for r in (1, 2, 3)]
    dquery, *key_parts = call(
        key_side_kernel,
        [((rows, 1536), bf16)] + parts_out,
        [table, docs, query, grad, totals, terms, *keys, *values],
        scratch=[whole, whole, window, window, bias, square, stack] + sums,
        cost=9, limit=28,
    )
    key_parts, w_got, messages = together((key_parts, w_got, messages))

    messages[1] = y_with(messages[1], 2)
    swapped = [core_swap(messages[0]), None, core_swap(messages[2])]
    key_parts[3], swapped = together((key_parts[3], swapped))
    arrived = [z_with(part, r + 1) for r, part in enumerate(key_parts[1:])]
    arrived[0], w_got = together((arrived[0], w_got))
    w_sum = w_got[0]
    for part in w_got[1:]:
        w_sum = w_sum + part.astype(f32)
    got = [
        first_with(w_sum[i * HEAD_SIZE : (i + 1) * HEAD_SIZE].astype(bf16), i) for i in (1, 2, 3)
    ]
    arrived, key_sum, slabs, messages, got[:2] = together(
        (arrived, key_parts[0], slabs, messages, got[:2])
    )
    for part in arrived:
        key_sum = key_sum + part.astype(f32)

    swapped[1] = core_swap(messages[1])
    key_rest = x_swap(key_sum[rows:].astype(bf16))
    (input_grad,) = call(
        input_kernel,
        [((rows, QUARTER), bf16)],
        [slabs, value_grads, own_rows, *messages, *swapped],
        scratch=[((QUARTER, 512), bf16), ((rows, 512), bf16), pltpu.SemaphoreType.DMA((10,))],
        anys=tuple(range(2, 9)),
        cost=4, limit=16,
    )
    got, input_grad, key_rest = together((got, input_grad, key_rest))
    key_grads = (key_sum[:rows] + key_rest.astype(f32)).astype(bf16)
    (weight_grad,) = call(
        functools.partial(fold_kernel, grad_scale),
        [((SLAB, HEAD_SIZE), f32)],
        [w_sum[:HEAD_SIZE], *got],
        smem=0,
    )
    return dquery[None], key_grads[None], input_grad[None], weight_grad


def solution(mesh):
    in_specs = (
        P("dp", "ctx", None),
        P("dp", "ctx", "head"),
        P("dp", "ctx", "head"),
        P(("dp", "ctx"), "head"),
        P("dp", "ctx", "head"),
        P("dp", "ctx", "head"),
        P("dp", None),
        P("dp", None),
    )
    out_specs = (
        P("dp", "ctx", "head"),
        P("dp", "ctx", "head"),
        P("dp", "ctx", "head"),
        P(("dp", "ctx"), "head"),
    )
    return jax.shard_map(local, mesh=mesh, in_specs=in_specs, out_specs=out_specs, check_vma=False)
```

```python
import functools

import jax
import jax.numpy as jnp
from jax import lax
from jax.experimental import pallas as pl
from jax.experimental.pallas import tpu as pltpu
from jax.sharding import PartitionSpec as P

HEAD_SIZE = 128
QUERY_PER_KEY = 12
PAIRS = QUERY_PER_KEY // 2
BLOCK = 128
WINDOW = 9
SPAN = WINDOW * BLOCK
SLAB = 384
QUARTER = 3072
HALF = QUARTER // 2
COST_UNIT = 3 << 20
MASKED = -1e30
LOG2E = 1.4426950408889634
SCALING = float(HEAD_SIZE) ** (-0.5)
f32 = jnp.float32
bf16 = jnp.bfloat16


def place_of(index):
    dp, ctx = divmod(index, 8)
    x_hi, core = divmod(dp, 2)
    x_lo, z = divmod(ctx, 4)
    return x_hi * 2 + x_lo, z, core


def index_of(x, z, core):
    x_hi, x_lo = divmod(x % 4, 2)
    return (x_hi * 2 + core) * 8 + x_lo * 4 + z % 4


def moved(value, where):
    pairs = [(i, index_of(*where(*place_of(i)))) for i in range(32)]
    return lax.ppermute(value, ("dp", "ctx"), pairs)


def core_swap(value):
    return moved(value, lambda x, z, c: (x, z, 1 - c))


def x_swap(value):
    return moved(value, lambda x, z, c: (x ^ 1, z, c))


def z_with(value, bits):
    return moved(value, lambda x, z, c: (x, z ^ bits, c))


def first_with(value, bits):
    return moved(value, lambda x, z, c: (x, z ^ bits, c) if c == 0 else (x ^ bits, z, c))


def second_with(value, bits):
    return moved(value, lambda x, z, c: (x ^ bits, z, c) if c == 0 else (x, z ^ bits, c))


def y_with(value, bits):
    return lax.ppermute(value, "head", [(y, y ^ bits) for y in range(4)])


def nt(a, b):
    return lax.dot_general(a, b, (((1,), (1,)), ((), ())), preferred_element_type=f32)


def nn(a, b):
    return lax.dot_general(a, b, (((1,), (0,)), ((), ())), preferred_element_type=f32)


def tn(a, b):
    return lax.dot_general(a, b, (((0,), (0,)), ((), ())), preferred_element_type=f32)


def row_terms_kernel(grad_ref, saved_ref, out_ref):
    for a in range(2):
        rows = slice(a * BLOCK, (a + 1) * BLOCK)
        for h in range(QUERY_PER_KEY):
            cols = slice(h * HEAD_SIZE, (h + 1) * HEAD_SIZE)
            product = grad_ref[rows, cols].astype(f32) * saved_ref[rows, cols].astype(f32)
            at = a * QUERY_PER_KEY + h
            out_ref[at : at + 1, :] = jnp.sum(product.T, axis=0, keepdims=True)


def join_kernel(own, *refs):
    parts, out, sem = refs[:-2], refs[-2], refs[-1]
    rows = parts[0].shape[0]
    copy = pltpu.make_async_copy(own, out.at[:rows, :], sem)
    copy.start()
    for i, part in enumerate(parts):
        out[(i + 1) * rows : (i + 2) * rows, :] = part[...]
    copy.wait()


def fold_kernel(scale, own, one, two, three, out):
    total = own[...] + one[...].astype(f32) + two[...].astype(f32) + three[...].astype(f32)
    out[...] = (total * scale).T


def fill_bias(place, doc_ref, bias_ref):
    docs = doc_ref[...]
    own = doc_ref[pl.ds(place, 1), :]
    start = jnp.zeros((1, BLOCK), f32)
    for d in range(1, 6):
        held = jnp.sum(jnp.where(docs == d - 1, 1.0, 0.0), axis=(0, 1), keepdims=True)
        start = start + jnp.where(own >= d, held, 0.0)
    start = start.astype(jnp.int32)
    query = place * BLOCK + lax.broadcasted_iota(jnp.int32, (1, BLOCK), 1)
    key = (place - (WINDOW - 1)) * BLOCK + lax.broadcasted_iota(jnp.int32, (SPAN, 1), 0)
    bias_ref[...] = jnp.where((key >= start) & (key <= query), 0.0, MASKED)


def fill_window(table_ref, place, parts, win_ref):
    for j in range(WINDOW):
        block = table_ref[jnp.maximum(place - (WINDOW - 1) + j, 0)]
        win_ref[j * BLOCK : (j + 1) * BLOCK, :] = parts[pl.ds(pl.multiple_of(block * BLOCK, BLOCK), BLOCK), :]


def join(parts, all_ref):
    rows = parts[0].shape[0]
    for i, part in enumerate(parts):
        all_ref[i * rows : (i + 1) * rows, :] = part[...]


def stacked(ref, a, pair):
    rows = slice(a * BLOCK, (a + 1) * BLOCK)
    one = ref[rows, pair * 256 : pair * 256 + 128]
    two = ref[rows, pair * 256 + 128 : pair * 256 + 256]
    return jnp.concatenate([one, two], axis=0)


def beside(ref, a, pair):
    at = a * QUERY_PER_KEY + 2 * pair
    return jnp.concatenate([ref[at : at + 1, :], ref[at + 1 : at + 2, :]], axis=1)


def add_window(table_ref, place, win_ref, sum_ref):
    for j in range(WINDOW):
        block = table_ref[jnp.maximum(place - (WINDOW - 1) + j, 0)]
        at = pl.ds(pl.multiple_of(block * BLOCK, BLOCK), BLOCK)
        sum_ref[at, :] += win_ref[j * BLOCK : (j + 1) * BLOCK, :]


def value_side_kernel(
    table_ref, doc_ref, q_any, g_any, k0, k1, k2, k3,
    total_ref, o0, o1, o2, o3,
    q_ref, g_ref, all_ref, win_ref, bias_ref, score_ref, raised_ref, scaled_ref, acc_ref, sum_ref, sems,
):
    copies = [
        pltpu.make_async_copy(q_any, q_ref, sems.at[0]),
        pltpu.make_async_copy(g_any, g_ref, sems.at[1]),
    ]
    for copy in copies:
        copy.start()
    join((k0, k1, k2, k3), all_ref)
    sum_ref[...] = jnp.zeros_like(sum_ref)
    for a in range(2):
        place = table_ref[16 + a]
        fill_bias(place, doc_ref, bias_ref)
        fill_window(table_ref, place, all_ref, win_ref)
        if a == 0:
            for copy in copies:
                copy.wait()
        for pair in range(PAIRS):
            cols = slice(pair * 256, (pair + 1) * 256)
            products = nt(win_ref[...], stacked(q_ref, a, pair))
            highest = None
            for j in range(WINDOW):
                keys = slice(j * BLOCK, (j + 1) * BLOCK)
                bias = jnp.concatenate([bias_ref[keys, :]] * 2, axis=1)
                scores = products[keys] * (SCALING * LOG2E) + bias
                score_ref[keys, :] = scores
                highest = scores if highest is None else jnp.maximum(highest, scores)
            highest = jnp.max(highest, axis=0, keepdims=True)
            total = None
            for j in range(WINDOW):
                keys = slice(j * BLOCK, (j + 1) * BLOCK)
                raised = jnp.exp2(score_ref[keys, :] - highest)
                total = raised if total is None else total + raised
                raised_ref[keys, cols] = raised.astype(bf16)
            total = jnp.sum(total, axis=0, keepdims=True)
            log_total = highest + jnp.log2(total)
            share = 1.0 / total
            for half in range(2):
                h = 2 * pair + half
                lanes = slice(half * BLOCK, (half + 1) * BLOCK)
                at = a * QUERY_PER_KEY + h
                total_ref[at : at + 1, :] = log_total[:, lanes]
                factor = jnp.broadcast_to(share[:, lanes], (BLOCK, BLOCK)).T
                grads = g_ref[a * BLOCK : (a + 1) * BLOCK, h * HEAD_SIZE : (h + 1) * HEAD_SIZE]
                scaled_ref[h * BLOCK : (h + 1) * BLOCK, :] = (grads.astype(f32) * factor).astype(bf16)
        acc_ref[...] = nn(raised_ref[...], scaled_ref[...])
        add_window(table_ref, place, acc_ref, sum_ref)
    o0[...] = sum_ref[0:512, :]
    for i, out in enumerate((o1, o2, o3)):
        out[...] = sum_ref[512 * (i + 1) : 512 * (i + 2), :].astype(bf16)


def key_side_kernel(
    table_ref, doc_ref, q_ref, g_ref, total_ref, term_ref, k0, k1, k2, k3, v0, v1, v2, v3,
    dq_ref, o0, o1, o2, o3,
    allk_ref, allv_ref, wink_ref, winv_ref, bias_ref, ds_ref, qs_ref, acc_ref, sum_ref,
):
    join((k0, k1, k2, k3), allk_ref)
    join((v0, v1, v2, v3), allv_ref)
    sum_ref[...] = jnp.zeros_like(sum_ref)
    for a in range(2):
        place = table_ref[16 + a]
        fill_bias(place, doc_ref, bias_ref)
        fill_window(table_ref, place, allk_ref, wink_ref)
        fill_window(table_ref, place, allv_ref, winv_ref)
        for pair in range(PAIRS):
            cols = slice(pair * 256, (pair + 1) * 256)
            query = stacked(q_ref, a, pair)
            qs_ref[cols, :] = query
            products = nt(wink_ref[...], query)
            dprobs = nt(winv_ref[...], stacked(g_ref, a, pair))
            log_total = beside(total_ref, a, pair)
            terms = beside(term_ref, a, pair)
            for j in range(WINDOW):
                keys = slice(j * BLOCK, (j + 1) * BLOCK)
                bias = jnp.concatenate([bias_ref[keys, :]] * 2, axis=1)
                probs = jnp.exp2(products[keys] * (SCALING * LOG2E) + bias - log_total)
                ds_ref[keys, cols] = (probs * (dprobs[keys] - terms)).astype(bf16)
        dquery = tn(wink_ref[...], ds_ref[...]) * SCALING
        for h in range(QUERY_PER_KEY):
            dq_ref[a * BLOCK : (a + 1) * BLOCK, h * HEAD_SIZE : (h + 1) * HEAD_SIZE] = (
                dquery[:, h * BLOCK : (h + 1) * BLOCK].T.astype(bf16)
            )
        acc_ref[...] = nn(ds_ref[...], qs_ref[...])
        add_window(table_ref, place, acc_ref, sum_ref)
    o0[...] = sum_ref[0:512, :] * SCALING
    for i, out in enumerate((o1, o2, o3)):
        out[...] = (sum_ref[512 * (i + 1) : 512 * (i + 2), :] * SCALING).astype(bf16)


def project_kernel(
    table_ref, hidden, w0, w1, w2, w3, s0, s1, s2, s3,
    out, own_rows, r1, r2, r3, hidden_ref, all_ref, sems,
):
    copies = [
        pltpu.make_async_copy(
            hidden.at[:, i * QUARTER : (i + 1) * QUARTER],
            hidden_ref.at[:, i * QUARTER : (i + 1) * QUARTER],
            sems.at[i],
        )
        for i in range(4)
    ]
    for copy in copies:
        copy.start()
    for k, w in enumerate((w0, w1, w2, w3, s0, s1, s2, s3)):
        for i in range(4):
            at = pl.multiple_of(table_ref[k * 4 + i] * SLAB, BLOCK)
            all_ref[pl.ds(at, SLAB), :] = w[i * SLAB : (i + 1) * SLAB, :]
    own_rows[...] = all_ref[pl.ds(pl.multiple_of(table_ref[32] * QUARTER, BLOCK), QUARTER), :]
    for d, r in enumerate((r1, r2, r3)):
        r[...] = all_ref[pl.ds(pl.multiple_of(table_ref[33 + d] * HALF, BLOCK), HALF), :]
    total = jnp.zeros(out.shape, f32)
    for i, copy in enumerate(copies):
        copy.wait()
        part = slice(i * QUARTER, (i + 1) * QUARTER)
        total = total + nn(hidden_ref[:, part], all_ref[part, :])
    out[...] = total.astype(bf16)


def weight_kernel(table_ref, hidden, grads, r1, r2, r3, own, other, m1, m2, m3):
    turned = grads[...].T
    for k in range(16):
        for out, at in ((other, 16 + k), (own, k)):
            cols = pl.ds(pl.multiple_of(table_ref[at] * SLAB, BLOCK), SLAB)
            block = nn(turned, hidden[:, cols])
            out[k * HEAD_SIZE : (k + 1) * HEAD_SIZE, :] = block.astype(out.dtype)
    for r, m in ((r1, m1), (r2, m2), (r3, m3)):
        m[:HALF, :] = r[...]
        m[HALF:, :] = grads[...]


def input_kernel(table_ref, grads, own, a1, a2, a3, b1, b2, b3, out, rows_ref, grads_ref, sems):
    mine = pl.multiple_of(table_ref[36] * HALF, BLOCK)
    other = pl.multiple_of((1 - table_ref[36]) * HALF, BLOCK)
    copies = [pltpu.make_async_copy(own, rows_ref.at[:, 0:BLOCK], sems.at[0])]
    for d, (a, b) in enumerate(((a1, b1), (a2, b2), (a3, b3))):
        cols = slice((d + 1) * BLOCK, (d + 2) * BLOCK)
        pieces = (
            (a.at[0:HALF, :], rows_ref.at[pl.ds(mine, HALF), cols]),
            (b.at[0:HALF, :], rows_ref.at[pl.ds(other, HALF), cols]),
            (a.at[HALF : HALF + 256, :], grads_ref.at[:, cols]),
        )
        for i, (source, target) in enumerate(pieces):
            copies.append(pltpu.make_async_copy(source, target, sems.at[3 * d + 1 + i]))
    for copy in copies:
        copy.start()
    grads_ref[:, 0:BLOCK] = grads[...]
    for copy in copies:
        copy.wait()
    for part in range(4):
        cols = slice(part * 768, (part + 1) * 768)
        out[:, cols] = nt(grads_ref[...], rows_ref[cols, :]).astype(bf16)


SMEM = pl.BlockSpec(memory_space=pltpu.SMEM)
VMEM = pl.BlockSpec(memory_space=pltpu.VMEM)


def call(kernel, outs, ins, scratch=(), cost=1, smem=1, anys=(), limit=8):
    any_spec = pl.BlockSpec(memory_space=pl.ANY)
    specs = [SMEM] * smem + [any_spec if i in anys else VMEM for i in range(smem, len(ins))]
    return pl.pallas_call(
        kernel,
        out_shape=tuple(jax.ShapeDtypeStruct(s, d) for s, d in outs),
        in_specs=specs,
        out_specs=tuple(VMEM for _ in outs),
        scratch_shapes=[s if not isinstance(s, tuple) else pltpu.VMEM(*s) for s in scratch],
        compiler_params=pltpu.CompilerParams(vmem_limit_bytes=limit * 1024 * 1024),
        cost_estimate=pl.CostEstimate(
            flops=0, bytes_accessed=int(cost * COST_UNIT), transcendentals=0
        ),
    )(*ins)


def joined(parts):
    rows = sum(part.shape[0] for part in parts)
    (whole,) = call(
        join_kernel,
        [((rows, HEAD_SIZE), bf16)],
        parts,
        scratch=[pltpu.SemaphoreType.DMA],
        smem=0, anys=(0,),
    )
    return whole


def summed_along_z(own, *parts):
    for r, part in enumerate(parts):
        own = own + z_with(part, r + 1).astype(f32)
    return own


def local(
    hidden_in,
    queries,
    rotary_key_rows,
    value_projection,
    output_gradient,
    attended,
    doc_ids,
    block_place,
):
    dp = lax.axis_index("dp")
    ctx = lax.axis_index("ctx")
    x_hi, core = dp // 2, dp % 2
    x_lo, z = ctx // 4, ctx % 4
    x = x_hi * 2 + x_lo
    rows = queries.shape[1]
    grad_scale = float(rows * 32) ** (-0.5)
    query, grad, saved = queries[0], output_gradient[0], attended[0]

    def places_of_keys(placing):
        stored = jnp.arange(16, dtype=jnp.int32)
        owner = stored // 2
        lies = ((owner % 4) ^ z) * 4 + ((owner // 4) ^ x_lo) * 2 + stored % 2
        by_place = jnp.sum(jnp.where(placing[None, :] == stored[:, None], lies[None, :], 0), axis=1)
        mine = jnp.sum(
            jnp.where(stored[None, :] == (2 * ctx + jnp.arange(2))[:, None], placing[None, :], 0), axis=1
        )
        return jnp.concatenate([by_place, mine])

    def places_of_slabs(head):
        outer, inner = jnp.arange(16, dtype=jnp.int32) // 4, jnp.arange(16, dtype=jnp.int32) % 4

        def slabs_of(core):
            at_x = x ^ jnp.where(core == 0, outer, inner)
            at_z = z ^ jnp.where(core == 0, inner, outer)
            return (2 * (at_x // 2) + core) * 8 + (at_x % 2) * 4 + at_z

        asked = jnp.stack([head] + [2 * (head ^ d) + core for d in (1, 2, 3)] + [core])
        return jnp.concatenate([slabs_of(core), slabs_of(1 - core), asked]).astype(jnp.int32)

    hidden = hidden_in[0]
    window = ((SPAN, HEAD_SIZE), bf16)
    whole = ((2048, HEAD_SIZE), bf16)
    bias = ((SPAN, BLOCK), f32)
    square = ((SPAN, 1536), bf16)
    stack = ((1536, HEAD_SIZE), bf16)
    sums = [((SPAN, HEAD_SIZE), f32), ((2048, HEAD_SIZE), f32)]
    parts_out = [((512, HEAD_SIZE), f32)] + [((512, HEAD_SIZE), bf16)] * 3
    together = lax.optimization_barrier

    own_keys = rotary_key_rows[0]
    lowest = jnp.finfo(bf16).min
    near, first, placing, head, docs = together(
        (
            [jnp.maximum(own_keys, lowest), x_swap(own_keys)],
            [jnp.maximum(value_projection, lowest)] + [first_with(value_projection, r) for r in (1, 2, 3)],
            block_place[0],
            lax.axis_index("head"),
            jnp.maximum(doc_ids[0], 0).reshape(16, BLOCK),
        )
    )
    near, first = joined(near), joined(first)

    keys, w1, w3, first, table, slabs, first_query = together(
        (
            [near] + [z_with(near, r) for r in (1, 2, 3)],
            second_with(first, 1),
            second_with(first, 3),
            first,
            places_of_keys(placing),
            places_of_slabs(head),
            jnp.maximum(query, lowest),
        )
    )

    w2 = second_with(w3, 1)
    s0, s1, s3 = core_swap(first), core_swap(w1), core_swap(w3)
    totals, *value_parts = call(
        value_side_kernel,
        [((24, 128), f32)] + parts_out,
        [table, docs, first_query, grad, *keys],
        scratch=[((rows, 1536), bf16)] * 2
        + [whole, window, bias, ((SPAN, 256), f32), square, stack]
        + sums
        + [pltpu.SemaphoreType.DMA((2,))],
        anys=(2, 3), cost=7, limit=48,
    )
    w2, s0, s1, s3, totals, value_parts, slabs = together((w2, s0, s1, s3, totals, value_parts, slabs))

    s2 = core_swap(w2)
    own_values, own_rows, *halves = call(
        project_kernel,
        [((rows, HEAD_SIZE), bf16), ((QUARTER, HEAD_SIZE), bf16)] + [((HALF, HEAD_SIZE), bf16)] * 3,
        [slabs, hidden, first, w1, w2, w3, s0, s1, s2, s3],
        scratch=[
            ((rows, 4 * QUARTER), bf16),
            ((4 * QUARTER, HEAD_SIZE), bf16),
            pltpu.SemaphoreType.DMA((4,)),
        ],
        anys=(1,), cost=4, limit=48,
    )
    arrived = [z_with(part, r + 1) for r, part in enumerate(value_parts[1:])]
    own_values, halves = together((own_values, halves))

    near_values, value_sum = together(([own_values, x_swap(own_values)], value_parts[0]))
    near_values = joined(near_values)
    for part in arrived:
        value_sum = value_sum + part.astype(f32)
    value_rest = x_swap(value_sum[rows:].astype(bf16))

    values = [near_values] + [z_with(near_values, r) for r in (1, 2, 3)]
    (terms,) = call(row_terms_kernel, [((24, 128), f32)], [grad, saved], smem=0)
    values, value_sum, value_rest, terms = together((values, value_sum, value_rest, terms))
    value_grads = (value_sum[:rows] + value_rest.astype(f32)).astype(bf16)

    message = ((HALF + rows, HEAD_SIZE), bf16)
    w_own, w_other, *messages = call(
        weight_kernel,
        [((2048, SLAB), f32), ((2048, SLAB), bf16)] + [message] * 3,
        [slabs, hidden, value_grads, *halves],
        cost=4, limit=24,
    )
    w_other = core_swap(w_other)
    w_parts = [
        w_own[512 * r : 512 * (r + 1)] + w_other[512 * r : 512 * (r + 1)].astype(f32) for r in range(4)
    ]
    w_parts = [w_parts[0]] + [part.astype(bf16) for part in w_parts[1:]]
    messages[0], messages[2] = y_with(messages[0], 1), y_with(messages[2], 3)
    w_got = [w_parts[0]] + [second_with(w_parts[r], r) for r in (1, 2, 3)]
    dquery, *key_parts = call(
        key_side_kernel,
        [((rows, 1536), bf16)] + parts_out,
        [table, docs, query, grad, totals, terms, *keys, *values],
        scratch=[whole, whole, window, window, bias, square, stack] + sums,
        cost=9, limit=28,
    )
    key_parts, w_got[:3], messages = together((key_parts, w_got[:3], messages))

    messages[1] = y_with(messages[1], 2)
    swapped = [core_swap(messages[0]), None, core_swap(messages[2])]
    key_parts[3], swapped = together((key_parts[3], swapped))
    arrived = [z_with(part, r + 1) for r, part in enumerate(key_parts[1:])]
    arrived[0], w_got = together((arrived[0], w_got))
    w_sum = w_got[0]
    for part in w_got[1:]:
        w_sum = w_sum + part.astype(f32)
    got = [
        first_with(w_sum[i * HEAD_SIZE : (i + 1) * HEAD_SIZE].astype(bf16), i) for i in (1, 2, 3)
    ]
    arrived, key_sum, slabs, messages, got[:2] = together(
        (arrived, key_parts[0], slabs, messages, got[:2])
    )
    for part in arrived:
        key_sum = key_sum + part.astype(f32)

    swapped[1] = core_swap(messages[1])
    key_rest = x_swap(key_sum[rows:].astype(bf16))
    (input_grad,) = call(
        input_kernel,
        [((rows, QUARTER), bf16)],
        [slabs, value_grads, own_rows, *messages, *swapped],
        scratch=[((QUARTER, 512), bf16), ((rows, 512), bf16), pltpu.SemaphoreType.DMA((10,))],
        anys=tuple(range(2, 9)),
        cost=4, limit=16,
    )
    got, input_grad, key_rest = together((got, input_grad, key_rest))
    key_grads = (key_sum[:rows] + key_rest.astype(f32)).astype(bf16)
    (weight_grad,) = call(
        functools.partial(fold_kernel, grad_scale),
        [((SLAB, HEAD_SIZE), f32)],
        [w_sum[:HEAD_SIZE], *got],
        smem=0,
    )
    return dquery[None], key_grads[None], input_grad[None], weight_grad


def solution(mesh):
    in_specs = (
        P("dp", "ctx", None),
        P("dp", "ctx", "head"),
        P("dp", "ctx", "head"),
        P(("dp", "ctx"), "head"),
        P("dp", "ctx", "head"),
        P("dp", "ctx", "head"),
        P("dp", None),
        P("dp", None),
    )
    out_specs = (
        P("dp", "ctx", "head"),
        P("dp", "ctx", "head"),
        P("dp", "ctx", "head"),
        P(("dp", "ctx"), "head"),
    )
    return jax.shard_map(local, mesh=mesh, in_specs=in_specs, out_specs=out_specs, check_vma=False)
```

```python
import functools

import jax
import jax.numpy as jnp
from jax import lax
from jax.experimental import pallas as pl
from jax.experimental.pallas import tpu as pltpu
from jax.sharding import PartitionSpec as P

HEAD_SIZE = 128
QUERY_PER_KEY = 12
PAIRS = QUERY_PER_KEY // 2
BLOCK = 128
WINDOW = 9
SPAN = WINDOW * BLOCK
SLAB = 384
QUARTER = 3072
HALF = QUARTER // 2
COST_UNIT = 3 << 20
MASKED = -1e30
LOG2E = 1.4426950408889634
SCALING = float(HEAD_SIZE) ** (-0.5)
f32 = jnp.float32
bf16 = jnp.bfloat16


def place_of(index):
    dp, ctx = divmod(index, 8)
    x_hi, core = divmod(dp, 2)
    x_lo, z = divmod(ctx, 4)
    return x_hi * 2 + x_lo, z, core


def index_of(x, z, core):
    x_hi, x_lo = divmod(x % 4, 2)
    return (x_hi * 2 + core) * 8 + x_lo * 4 + z % 4


def moved(value, where):
    pairs = [(i, index_of(*where(*place_of(i)))) for i in range(32)]
    return lax.ppermute(value, ("dp", "ctx"), pairs)


def core_swap(value):
    return moved(value, lambda x, z, c: (x, z, 1 - c))


def x_swap(value):
    return moved(value, lambda x, z, c: (x ^ 1, z, c))


def z_with(value, bits):
    return moved(value, lambda x, z, c: (x, z ^ bits, c))


def first_with(value, bits):
    return moved(value, lambda x, z, c: (x, z ^ bits, c) if c == 0 else (x ^ bits, z, c))


def second_with(value, bits):
    return moved(value, lambda x, z, c: (x ^ bits, z, c) if c == 0 else (x, z ^ bits, c))


def y_with(value, bits):
    return lax.ppermute(value, "head", [(y, y ^ bits) for y in range(4)])


def nt(a, b):
    return lax.dot_general(a, b, (((1,), (1,)), ((), ())), preferred_element_type=f32)


def nn(a, b):
    return lax.dot_general(a, b, (((1,), (0,)), ((), ())), preferred_element_type=f32)


def tn(a, b):
    return lax.dot_general(a, b, (((0,), (0,)), ((), ())), preferred_element_type=f32)


def row_terms_kernel(grad_ref, saved_ref, out_ref):
    for a in range(2):
        rows = slice(a * BLOCK, (a + 1) * BLOCK)
        for h in range(QUERY_PER_KEY):
            cols = slice(h * HEAD_SIZE, (h + 1) * HEAD_SIZE)
            product = grad_ref[rows, cols].astype(f32) * saved_ref[rows, cols].astype(f32)
            at = a * QUERY_PER_KEY + h
            out_ref[at : at + 1, :] = jnp.sum(product.T, axis=0, keepdims=True)


def join_kernel(own, *refs):
    parts, out, sem = refs[:-2], refs[-2], refs[-1]
    rows = parts[0].shape[0]
    copy = pltpu.make_async_copy(own, out.at[:rows, :], sem)
    copy.start()
    for i, part in enumerate(parts):
        out[(i + 1) * rows : (i + 2) * rows, :] = part[...]
    copy.wait()


def fold_kernel(scale, own, one, two, three, out):
    total = own[...] + one[...].astype(f32) + two[...].astype(f32) + three[...].astype(f32)
    out[...] = (total * scale).T


def fill_bias(place, doc_ref, bias_ref):
    docs = doc_ref[...]
    own = doc_ref[pl.ds(place, 1), :]
    start = jnp.zeros((1, BLOCK), f32)
    for d in range(1, 6):
        held = jnp.sum(jnp.where(docs == d - 1, 1.0, 0.0), axis=(0, 1), keepdims=True)
        start = start + jnp.where(own >= d, held, 0.0)
    start = start.astype(jnp.int32)
    query = place * BLOCK + lax.broadcasted_iota(jnp.int32, (1, BLOCK), 1)
    key = (place - (WINDOW - 1)) * BLOCK + lax.broadcasted_iota(jnp.int32, (SPAN, 1), 0)
    bias_ref[...] = jnp.where((key >= start) & (key <= query), 0.0, MASKED)


def fill_window(table_ref, place, parts, win_ref):
    for j in range(WINDOW):
        block = table_ref[jnp.maximum(place - (WINDOW - 1) + j, 0)]
        win_ref[j * BLOCK : (j + 1) * BLOCK, :] = parts[pl.ds(pl.multiple_of(block * BLOCK, BLOCK), BLOCK), :]


def join(parts, all_ref):
    rows = parts[0].shape[0]
    for i, part in enumerate(parts):
        all_ref[i * rows : (i + 1) * rows, :] = part[...]


def stacked(ref, a, pair):
    rows = slice(a * BLOCK, (a + 1) * BLOCK)
    one = ref[rows, pair * 256 : pair * 256 + 128]
    two = ref[rows, pair * 256 + 128 : pair * 256 + 256]
    return jnp.concatenate([one, two], axis=0)


def beside(ref, a, pair):
    at = a * QUERY_PER_KEY + 2 * pair
    return jnp.concatenate([ref[at : at + 1, :], ref[at + 1 : at + 2, :]], axis=1)


def add_window(table_ref, place, win_ref, sum_ref):
    for j in range(WINDOW):
        block = table_ref[jnp.maximum(place - (WINDOW - 1) + j, 0)]
        at = pl.ds(pl.multiple_of(block * BLOCK, BLOCK), BLOCK)
        sum_ref[at, :] += win_ref[j * BLOCK : (j + 1) * BLOCK, :]


def value_side_kernel(
    table_ref, doc_ref, q_any, g_any, k0, k1, k2, k3,
    total_ref, o0, o1, o2, o3,
    q_ref, g_ref, all_ref, win_ref, bias_ref, score_ref, raised_ref, scaled_ref, acc_ref, sum_ref, sems,
):
    copies = [
        pltpu.make_async_copy(q_any, q_ref, sems.at[0]),
        pltpu.make_async_copy(g_any, g_ref, sems.at[1]),
    ]
    for copy in copies:
        copy.start()
    join((k0, k1, k2, k3), all_ref)
    sum_ref[...] = jnp.zeros_like(sum_ref)
    for a in range(2):
        place = table_ref[16 + a]
        fill_bias(place, doc_ref, bias_ref)
        fill_window(table_ref, place, all_ref, win_ref)
        if a == 0:
            for copy in copies:
                copy.wait()
        for pair in range(PAIRS):
            cols = slice(pair * 256, (pair + 1) * 256)
            products = nt(win_ref[...], stacked(q_ref, a, pair))
            highest = None
            for j in range(WINDOW):
                keys = slice(j * BLOCK, (j + 1) * BLOCK)
                bias = jnp.concatenate([bias_ref[keys, :]] * 2, axis=1)
                scores = products[keys] * (SCALING * LOG2E) + bias
                score_ref[keys, :] = scores
                highest = scores if highest is None else jnp.maximum(highest, scores)
            highest = jnp.max(highest, axis=0, keepdims=True)
            total = None
            for j in range(WINDOW):
                keys = slice(j * BLOCK, (j + 1) * BLOCK)
                raised = jnp.exp2(score_ref[keys, :] - highest)
                total = raised if total is None else total + raised
                raised_ref[keys, cols] = raised.astype(bf16)
            total = jnp.sum(total, axis=0, keepdims=True)
            log_total = highest + jnp.log2(total)
            share = 1.0 / total
            for half in range(2):
                h = 2 * pair + half
                lanes = slice(half * BLOCK, (half + 1) * BLOCK)
                at = a * QUERY_PER_KEY + h
                total_ref[at : at + 1, :] = log_total[:, lanes]
                factor = jnp.broadcast_to(share[:, lanes], (BLOCK, BLOCK)).T
                grads = g_ref[a * BLOCK : (a + 1) * BLOCK, h * HEAD_SIZE : (h + 1) * HEAD_SIZE]
                scaled_ref[h * BLOCK : (h + 1) * BLOCK, :] = (grads.astype(f32) * factor).astype(bf16)
        acc_ref[...] = nn(raised_ref[...], scaled_ref[...])
        add_window(table_ref, place, acc_ref, sum_ref)
    o0[...] = sum_ref[0:512, :]
    for i, out in enumerate((o1, o2, o3)):
        out[...] = sum_ref[512 * (i + 1) : 512 * (i + 2), :].astype(bf16)


def key_side_kernel(
    table_ref, doc_ref, q_ref, g_ref, total_ref, term_ref, k0, k1, k2, k3, v0, v1, v2, v3,
    dq_ref, o0, o1, o2, o3,
    allk_ref, allv_ref, wink_ref, winv_ref, bias_ref, ds_ref, qs_ref, acc_ref, sum_ref,
):
    join((k0, k1, k2, k3), allk_ref)
    join((v0, v1, v2, v3), allv_ref)
    sum_ref[...] = jnp.zeros_like(sum_ref)
    for a in range(2):
        place = table_ref[16 + a]
        fill_bias(place, doc_ref, bias_ref)
        fill_window(table_ref, place, allk_ref, wink_ref)
        fill_window(table_ref, place, allv_ref, winv_ref)
        for pair in range(PAIRS):
            cols = slice(pair * 256, (pair + 1) * 256)
            query = stacked(q_ref, a, pair)
            qs_ref[cols, :] = query
            products = nt(wink_ref[...], query)
            dprobs = nt(winv_ref[...], stacked(g_ref, a, pair))
            log_total = beside(total_ref, a, pair)
            terms = beside(term_ref, a, pair)
            for j in range(WINDOW):
                keys = slice(j * BLOCK, (j + 1) * BLOCK)
                bias = jnp.concatenate([bias_ref[keys, :]] * 2, axis=1)
                probs = jnp.exp2(products[keys] * (SCALING * LOG2E) + bias - log_total)
                ds_ref[keys, cols] = (probs * (dprobs[keys] - terms)).astype(bf16)
        dquery = tn(wink_ref[...], ds_ref[...]) * SCALING
        for h in range(QUERY_PER_KEY):
            dq_ref[a * BLOCK : (a + 1) * BLOCK, h * HEAD_SIZE : (h + 1) * HEAD_SIZE] = (
                dquery[:, h * BLOCK : (h + 1) * BLOCK].T.astype(bf16)
            )
        acc_ref[...] = nn(ds_ref[...], qs_ref[...])
        add_window(table_ref, place, acc_ref, sum_ref)
    o0[...] = sum_ref[0:512, :] * SCALING
    for i, out in enumerate((o1, o2, o3)):
        out[...] = (sum_ref[512 * (i + 1) : 512 * (i + 2), :] * SCALING).astype(bf16)


def project_kernel(
    table_ref, hidden, w0, w1, w2, w3, s0, s1, s2, s3,
    out, own_rows, r1, r2, r3, hidden_ref, all_ref, sems,
):
    copies = [
        pltpu.make_async_copy(
            hidden.at[:, i * QUARTER : (i + 1) * QUARTER],
            hidden_ref.at[:, i * QUARTER : (i + 1) * QUARTER],
            sems.at[i],
        )
        for i in range(4)
    ]
    for copy in copies:
        copy.start()
    for k, w in enumerate((w0, w1, w2, w3, s0, s1, s2, s3)):
        for i in range(4):
            at = pl.multiple_of(table_ref[k * 4 + i] * SLAB, BLOCK)
            all_ref[pl.ds(at, SLAB), :] = w[i * SLAB : (i + 1) * SLAB, :]
    own_rows[...] = all_ref[pl.ds(pl.multiple_of(table_ref[32] * QUARTER, BLOCK), QUARTER), :]
    for d, r in enumerate((r1, r2, r3)):
        r[...] = all_ref[pl.ds(pl.multiple_of(table_ref[33 + d] * HALF, BLOCK), HALF), :]
    total = jnp.zeros(out.shape, f32)
    for i, copy in enumerate(copies):
        copy.wait()
        part = slice(i * QUARTER, (i + 1) * QUARTER)
        total = total + nn(hidden_ref[:, part], all_ref[part, :])
    out[...] = total.astype(bf16)


def weight_kernel(table_ref, hidden, grads, r1, r2, r3, own, other, m1, m2, m3):
    turned = grads[...].T
    for k in range(16):
        for out, at in ((other, 16 + k), (own, k)):
            cols = pl.ds(pl.multiple_of(table_ref[at] * SLAB, BLOCK), SLAB)
            block = nn(turned, hidden[:, cols])
            out[k * HEAD_SIZE : (k + 1) * HEAD_SIZE, :] = block.astype(out.dtype)
    for r, m in ((r1, m1), (r2, m2), (r3, m3)):
        m[:HALF, :] = r[...]
        m[HALF:, :] = grads[...]


def input_kernel(table_ref, grads, own, a1, a2, a3, b1, b2, b3, out, rows_ref, grads_ref, sems):
    mine = pl.multiple_of(table_ref[36] * HALF, BLOCK)
    other = pl.multiple_of((1 - table_ref[36]) * HALF, BLOCK)
    copies = [pltpu.make_async_copy(own, rows_ref.at[:, 0:BLOCK], sems.at[0])]
    for d, (a, b) in enumerate(((a1, b1), (a2, b2), (a3, b3))):
        cols = slice((d + 1) * BLOCK, (d + 2) * BLOCK)
        pieces = (
            (a.at[0:HALF, :], rows_ref.at[pl.ds(mine, HALF), cols]),
            (b.at[0:HALF, :], rows_ref.at[pl.ds(other, HALF), cols]),
            (a.at[HALF : HALF + 256, :], grads_ref.at[:, cols]),
        )
        for i, (source, target) in enumerate(pieces):
            copies.append(pltpu.make_async_copy(source, target, sems.at[3 * d + 1 + i]))
    for copy in copies:
        copy.start()
    grads_ref[:, 0:BLOCK] = grads[...]
    for copy in copies:
        copy.wait()
    for part in range(4):
        cols = slice(part * 768, (part + 1) * 768)
        out[:, cols] = nt(grads_ref[...], rows_ref[cols, :]).astype(bf16)


SMEM = pl.BlockSpec(memory_space=pltpu.SMEM)
VMEM = pl.BlockSpec(memory_space=pltpu.VMEM)


def call(kernel, outs, ins, scratch=(), cost=1, smem=1, anys=(), limit=8):
    any_spec = pl.BlockSpec(memory_space=pl.ANY)
    specs = [SMEM] * smem + [any_spec if i in anys else VMEM for i in range(smem, len(ins))]
    return pl.pallas_call(
        kernel,
        out_shape=tuple(jax.ShapeDtypeStruct(s, d) for s, d in outs),
        in_specs=specs,
        out_specs=tuple(VMEM for _ in outs),
        scratch_shapes=[s if not isinstance(s, tuple) else pltpu.VMEM(*s) for s in scratch],
        compiler_params=pltpu.CompilerParams(vmem_limit_bytes=limit * 1024 * 1024),
        cost_estimate=pl.CostEstimate(
            flops=0, bytes_accessed=int(cost * COST_UNIT), transcendentals=0
        ),
    )(*ins)


def joined(parts):
    rows = sum(part.shape[0] for part in parts)
    (whole,) = call(
        join_kernel,
        [((rows, HEAD_SIZE), bf16)],
        parts,
        scratch=[pltpu.SemaphoreType.DMA],
        smem=0, anys=(0,),
    )
    return whole


def summed_along_z(own, *parts):
    for r, part in enumerate(parts):
        own = own + z_with(part, r + 1).astype(f32)
    return own


def local(
    hidden_in,
    queries,
    rotary_key_rows,
    value_projection,
    output_gradient,
    attended,
    doc_ids,
    block_place,
):
    dp = lax.axis_index("dp")
    ctx = lax.axis_index("ctx")
    x_hi, core = dp // 2, dp % 2
    x_lo, z = ctx // 4, ctx % 4
    x = x_hi * 2 + x_lo
    rows = queries.shape[1]
    grad_scale = float(rows * 32) ** (-0.5)
    query, grad, saved = queries[0], output_gradient[0], attended[0]

    def places_of_keys(placing):
        stored = jnp.arange(16, dtype=jnp.int32)
        owner = stored // 2
        lies = ((owner % 4) ^ z) * 4 + ((owner // 4) ^ x_lo) * 2 + stored % 2
        by_place = jnp.sum(jnp.where(placing[None, :] == stored[:, None], lies[None, :], 0), axis=1)
        mine = jnp.sum(
            jnp.where(stored[None, :] == (2 * ctx + jnp.arange(2))[:, None], placing[None, :], 0), axis=1
        )
        return jnp.concatenate([by_place, mine])

    def places_of_slabs(head):
        outer, inner = jnp.arange(16, dtype=jnp.int32) // 4, jnp.arange(16, dtype=jnp.int32) % 4

        def slabs_of(core):
            at_x = x ^ jnp.where(core == 0, outer, inner)
            at_z = z ^ jnp.where(core == 0, inner, outer)
            return (2 * (at_x // 2) + core) * 8 + (at_x % 2) * 4 + at_z

        asked = jnp.stack([head] + [2 * (head ^ d) + core for d in (1, 2, 3)] + [core])
        return jnp.concatenate([slabs_of(core), slabs_of(1 - core), asked]).astype(jnp.int32)

    hidden = hidden_in[0]
    window = ((SPAN, HEAD_SIZE), bf16)
    whole = ((2048, HEAD_SIZE), bf16)
    bias = ((SPAN, BLOCK), f32)
    square = ((SPAN, 1536), bf16)
    stack = ((1536, HEAD_SIZE), bf16)
    sums = [((SPAN, HEAD_SIZE), f32), ((2048, HEAD_SIZE), f32)]
    parts_out = [((512, HEAD_SIZE), f32)] + [((512, HEAD_SIZE), bf16)] * 3
    together = lax.optimization_barrier

    own_keys = rotary_key_rows[0]
    lowest = jnp.finfo(bf16).min
    near, first, placing, head, docs = together(
        (
            [jnp.maximum(own_keys, lowest), x_swap(own_keys)],
            [jnp.maximum(value_projection, lowest)] + [first_with(value_projection, r) for r in (1, 2, 3)],
            block_place[0],
            lax.axis_index("head"),
            jnp.maximum(doc_ids[0], 0).reshape(16, BLOCK),
        )
    )
    near, first = joined(near), joined(first)

    keys, w1, w3, first, table, slabs, first_query = together(
        (
            [near] + [z_with(near, r) for r in (1, 2, 3)],
            second_with(first, 1),
            second_with(first, 3),
            first,
            places_of_keys(placing),
            places_of_slabs(head),
            jnp.maximum(query, lowest),
        )
    )

    w2 = second_with(w3, 1)
    s0, s1, s3 = core_swap(first), core_swap(w1), core_swap(w3)
    totals, *value_parts = call(
        value_side_kernel,
        [((24, 128), f32)] + parts_out,
        [table, docs, first_query, grad, *keys],
        scratch=[((rows, 1536), bf16)] * 2
        + [whole, window, bias, ((SPAN, 256), f32), square, stack]
        + sums
        + [pltpu.SemaphoreType.DMA((2,))],
        anys=(2, 3), cost=7, limit=48,
    )
    w2, s0, s1, s3, totals, value_parts, slabs = together((w2, s0, s1, s3, totals, value_parts, slabs))

    s2 = core_swap(w2)
    own_values, own_rows, *halves = call(
        project_kernel,
        [((rows, HEAD_SIZE), bf16), ((QUARTER, HEAD_SIZE), bf16)] + [((HALF, HEAD_SIZE), bf16)] * 3,
        [slabs, hidden, first, w1, w2, w3, s0, s1, s2, s3],
        scratch=[
            ((rows, 4 * QUARTER), bf16),
            ((4 * QUARTER, HEAD_SIZE), bf16),
            pltpu.SemaphoreType.DMA((4,)),
        ],
        anys=(1,), cost=4, limit=48,
    )
    arrived = [z_with(part, r + 1) for r, part in enumerate(value_parts[1:])]
    own_values, halves = together((own_values, halves))

    near_values, value_sum = together(([own_values, x_swap(own_values)], value_parts[0]))
    near_values = joined(near_values)
    for part in arrived:
        value_sum = value_sum + part.astype(f32)
    value_rest = x_swap(value_sum.astype(bf16))[rows:]

    values = [near_values] + [z_with(near_values, r) for r in (1, 2, 3)]
    (terms,) = call(row_terms_kernel, [((24, 128), f32)], [grad, saved], smem=0)
    value_grads = (value_sum[:rows] + value_rest.astype(f32)).astype(bf16)

    message = ((HALF + rows, HEAD_SIZE), bf16)
    w_own, w_other, *messages = call(
        weight_kernel,
        [((2048, SLAB), f32), ((2048, SLAB), bf16)] + [message] * 3,
        [slabs, hidden, value_grads, *halves],
        cost=4, limit=24,
    )
    values, terms, w_own, w_other, messages, value_grads = together(
        (values, terms, w_own, w_other, messages, value_grads)
    )

    w_other = core_swap(w_other)
    w_parts = [
        w_own[512 * r : 512 * (r + 1)] + w_other[512 * r : 512 * (r + 1)].astype(f32) for r in range(4)
    ]
    w_parts = [w_parts[0]] + [part.astype(bf16) for part in w_parts[1:]]
    messages[0], messages[2] = y_with(messages[0], 1), y_with(messages[2], 3)
    w_got = [w_parts[0]] + [second_with(w_parts[r], r) for r in (1, 2, 3)]
    dquery, *key_parts = call(
        key_side_kernel,
        [((rows, 1536), bf16)] + parts_out,
        [table, docs, query, grad, totals, terms, *keys, *values],
        scratch=[whole, whole, window, window, bias, square, stack] + sums,
        cost=9, limit=28,
    )
    key_parts, w_got[:3], messages = together((key_parts, w_got[:3], messages))

    messages[1] = y_with(messages[1], 2)
    swapped = [core_swap(messages[0]), None, core_swap(messages[2])]
    key_parts[3], swapped = together((key_parts[3], swapped))
    arrived = [z_with(part, r + 1) for r, part in enumerate(key_parts[1:])]
    arrived[0], w_got = together((arrived[0], w_got))
    w_sum = w_got[0]
    for part in w_got[1:]:
        w_sum = w_sum + part.astype(f32)
    got = [
        first_with(w_sum[i * HEAD_SIZE : (i + 1) * HEAD_SIZE].astype(bf16), i) for i in (1, 2, 3)
    ]
    arrived, key_sum, slabs, messages, got[:2] = together(
        (arrived, key_parts[0], slabs, messages, got[:2])
    )
    for part in arrived:
        key_sum = key_sum + part.astype(f32)

    swapped[1] = core_swap(messages[1])
    key_rest = x_swap(key_sum[rows:].astype(bf16))
    (input_grad,) = call(
        input_kernel,
        [((rows, QUARTER), bf16)],
        [slabs, value_grads, own_rows, *messages, *swapped],
        scratch=[((QUARTER, 512), bf16), ((rows, 512), bf16), pltpu.SemaphoreType.DMA((10,))],
        anys=tuple(range(2, 9)),
        cost=4, limit=16,
    )
    got, input_grad, key_rest = together((got, input_grad, key_rest))
    key_grads = (key_sum[:rows] + key_rest.astype(f32)).astype(bf16)
    (weight_grad,) = call(
        functools.partial(fold_kernel, grad_scale),
        [((SLAB, HEAD_SIZE), f32)],
        [w_sum[:HEAD_SIZE], *got],
        smem=0,
    )
    return dquery[None], key_grads[None], input_grad[None], weight_grad


def solution(mesh):
    in_specs = (
        P("dp", "ctx", None),
        P("dp", "ctx", "head"),
        P("dp", "ctx", "head"),
        P(("dp", "ctx"), "head"),
        P("dp", "ctx", "head"),
        P("dp", "ctx", "head"),
        P("dp", None),
        P("dp", None),
    )
    out_specs = (
        P("dp", "ctx", "head"),
        P("dp", "ctx", "head"),
        P("dp", "ctx", "head"),
        P(("dp", "ctx"), "head"),
    )
    return jax.shard_map(local, mesh=mesh, in_specs=in_specs, out_specs=out_specs, check_vma=False)
```

```python
import functools

import jax
import jax.numpy as jnp
from jax import lax
from jax.experimental import pallas as pl
from jax.experimental.pallas import tpu as pltpu
from jax.sharding import PartitionSpec as P

HEAD_SIZE = 128
QUERY_PER_KEY = 12
PAIRS = QUERY_PER_KEY // 2
BLOCK = 128
WINDOW = 9
SPAN = WINDOW * BLOCK
SLAB = 384
QUARTER = 3072
HALF = QUARTER // 2
COST_UNIT = 3 << 20
MASKED = -1e30
LOG2E = 1.4426950408889634
SCALING = float(HEAD_SIZE) ** (-0.5)
f32 = jnp.float32
bf16 = jnp.bfloat16


def place_of(index):
    dp, ctx = divmod(index, 8)
    x_hi, core = divmod(dp, 2)
    x_lo, z = divmod(ctx, 4)
    return x_hi * 2 + x_lo, z, core


def index_of(x, z, core):
    x_hi, x_lo = divmod(x % 4, 2)
    return (x_hi * 2 + core) * 8 + x_lo * 4 + z % 4


def moved(value, where):
    pairs = [(i, index_of(*where(*place_of(i)))) for i in range(32)]
    return lax.ppermute(value, ("dp", "ctx"), pairs)


def core_swap(value):
    return moved(value, lambda x, z, c: (x, z, 1 - c))


def x_swap(value):
    return moved(value, lambda x, z, c: (x ^ 1, z, c))


def z_with(value, bits):
    return moved(value, lambda x, z, c: (x, z ^ bits, c))


def first_with(value, bits):
    return moved(value, lambda x, z, c: (x, z ^ bits, c) if c == 0 else (x ^ bits, z, c))


def second_with(value, bits):
    return moved(value, lambda x, z, c: (x ^ bits, z, c) if c == 0 else (x, z ^ bits, c))


def y_with(value, bits):
    return lax.ppermute(value, "head", [(y, y ^ bits) for y in range(4)])


def nt(a, b):
    return lax.dot_general(a, b, (((1,), (1,)), ((), ())), preferred_element_type=f32)


def nn(a, b):
    return lax.dot_general(a, b, (((1,), (0,)), ((), ())), preferred_element_type=f32)


def tn(a, b):
    return lax.dot_general(a, b, (((0,), (0,)), ((), ())), preferred_element_type=f32)


def row_terms_kernel(grad_ref, saved_ref, out_ref):
    for a in range(2):
        rows = slice(a * BLOCK, (a + 1) * BLOCK)
        for h in range(QUERY_PER_KEY):
            cols = slice(h * HEAD_SIZE, (h + 1) * HEAD_SIZE)
            product = grad_ref[rows, cols].astype(f32) * saved_ref[rows, cols].astype(f32)
            at = a * QUERY_PER_KEY + h
            out_ref[at : at + 1, :] = jnp.sum(product.T, axis=0, keepdims=True)


def join_kernel(own, *refs):
    parts, out, sem = refs[:-2], refs[-2], refs[-1]
    rows = parts[0].shape[0]
    copy = pltpu.make_async_copy(own, out.at[:rows, :], sem)
    copy.start()
    for i, part in enumerate(parts):
        out[(i + 1) * rows : (i + 2) * rows, :] = part[...]
    copy.wait()


def fold_kernel(scale, own, one, two, three, out):
    total = own[...] + one[...].astype(f32) + two[...].astype(f32) + three[...].astype(f32)
    out[...] = (total * scale).T


def fill_bias(place, doc_ref, bias_ref):
    docs = doc_ref[...]
    own = doc_ref[pl.ds(place, 1), :]
    start = jnp.zeros((1, BLOCK), f32)
    for d in range(1, 6):
        held = jnp.sum(jnp.where(docs == d - 1, 1.0, 0.0), axis=(0, 1), keepdims=True)
        start = start + jnp.where(own >= d, held, 0.0)
    start = start.astype(jnp.int32)
    query = place * BLOCK + lax.broadcasted_iota(jnp.int32, (1, BLOCK), 1)
    key = (place - (WINDOW - 1)) * BLOCK + lax.broadcasted_iota(jnp.int32, (SPAN, 1), 0)
    bias_ref[...] = jnp.where((key >= start) & (key <= query), 0.0, MASKED)


def fill_window(table_ref, place, parts, win_ref):
    for j in range(WINDOW):
        block = table_ref[jnp.maximum(place - (WINDOW - 1) + j, 0)]
        win_ref[j * BLOCK : (j + 1) * BLOCK, :] = parts[pl.ds(pl.multiple_of(block * BLOCK, BLOCK), BLOCK), :]


def join(parts, all_ref):
    rows = parts[0].shape[0]
    for i, part in enumerate(parts):
        all_ref[i * rows : (i + 1) * rows, :] = part[...]


def stacked(ref, a, pair):
    rows = slice(a * BLOCK, (a + 1) * BLOCK)
    one = ref[rows, pair * 256 : pair * 256 + 128]
    two = ref[rows, pair * 256 + 128 : pair * 256 + 256]
    return jnp.concatenate([one, two], axis=0)


def beside(ref, a, pair):
    at = a * QUERY_PER_KEY + 2 * pair
    return jnp.concatenate([ref[at : at + 1, :], ref[at + 1 : at + 2, :]], axis=1)


def add_window(table_ref, place, win_ref, sum_ref):
    for j in range(WINDOW):
        block = table_ref[jnp.maximum(place - (WINDOW - 1) + j, 0)]
        at = pl.ds(pl.multiple_of(block * BLOCK, BLOCK), BLOCK)
        sum_ref[at, :] += win_ref[j * BLOCK : (j + 1) * BLOCK, :]


def value_side_kernel(
    table_ref, doc_ref, q_any, g_any, k0, k1, k2, k3,
    total_ref, o0, o1, o2, o3,
    q_ref, g_ref, all_ref, win_ref, bias_ref, score_ref, raised_ref, scaled_ref, acc_ref, sum_ref, sems,
):
    copies = [
        pltpu.make_async_copy(q_any, q_ref, sems.at[0]),
        pltpu.make_async_copy(g_any, g_ref, sems.at[1]),
    ]
    for copy in copies:
        copy.start()
    join((k0, k1, k2, k3), all_ref)
    sum_ref[...] = jnp.zeros_like(sum_ref)
    for a in range(2):
        place = table_ref[16 + a]
        fill_bias(place, doc_ref, bias_ref)
        fill_window(table_ref, place, all_ref, win_ref)
        if a == 0:
            for copy in copies:
                copy.wait()
        for pair in range(PAIRS):
            cols = slice(pair * 256, (pair + 1) * 256)
            products = nt(win_ref[...], stacked(q_ref, a, pair))
            highest = None
            for j in range(WINDOW):
                keys = slice(j * BLOCK, (j + 1) * BLOCK)
                bias = jnp.concatenate([bias_ref[keys, :]] * 2, axis=1)
                scores = products[keys] * (SCALING * LOG2E) + bias
                score_ref[keys, :] = scores
                highest = scores if highest is None else jnp.maximum(highest, scores)
            highest = jnp.max(highest, axis=0, keepdims=True)
            total = None
            for j in range(WINDOW):
                keys = slice(j * BLOCK, (j + 1) * BLOCK)
                raised = jnp.exp2(score_ref[keys, :] - highest)
                total = raised if total is None else total + raised
                raised_ref[keys, cols] = raised.astype(bf16)
            total = jnp.sum(total, axis=0, keepdims=True)
            log_total = highest + jnp.log2(total)
            share = 1.0 / total
            for half in range(2):
                h = 2 * pair + half
                lanes = slice(half * BLOCK, (half + 1) * BLOCK)
                at = a * QUERY_PER_KEY + h
                total_ref[at : at + 1, :] = log_total[:, lanes]
                factor = jnp.broadcast_to(share[:, lanes], (BLOCK, BLOCK)).T
                grads = g_ref[a * BLOCK : (a + 1) * BLOCK, h * HEAD_SIZE : (h + 1) * HEAD_SIZE]
                scaled_ref[h * BLOCK : (h + 1) * BLOCK, :] = (grads.astype(f32) * factor).astype(bf16)
        acc_ref[...] = nn(raised_ref[...], scaled_ref[...])
        add_window(table_ref, place, acc_ref, sum_ref)
    o0[...] = sum_ref[0:512, :]
    for i, out in enumerate((o1, o2, o3)):
        out[...] = sum_ref[512 * (i + 1) : 512 * (i + 2), :].astype(bf16)


def key_side_kernel(
    table_ref, doc_ref, q_ref, g_ref, total_ref, term_ref, k0, k1, k2, k3, v0, v1, v2, v3,
    dq_ref, o0, o1, o2, o3,
    allk_ref, allv_ref, wink_ref, winv_ref, bias_ref, ds_ref, qs_ref, acc_ref, sum_ref,
):
    join((k0, k1, k2, k3), allk_ref)
    join((v0, v1, v2, v3), allv_ref)
    sum_ref[...] = jnp.zeros_like(sum_ref)
    for a in range(2):
        place = table_ref[16 + a]
        fill_bias(place, doc_ref, bias_ref)
        fill_window(table_ref, place, allk_ref, wink_ref)
        fill_window(table_ref, place, allv_ref, winv_ref)
        for pair in range(PAIRS):
            cols = slice(pair * 256, (pair + 1) * 256)
            query = stacked(q_ref, a, pair)
            qs_ref[cols, :] = query
            products = nt(wink_ref[...], query)
            dprobs = nt(winv_ref[...], stacked(g_ref, a, pair))
            log_total = beside(total_ref, a, pair)
            terms = beside(term_ref, a, pair)
            for j in range(WINDOW):
                keys = slice(j * BLOCK, (j + 1) * BLOCK)
                bias = jnp.concatenate([bias_ref[keys, :]] * 2, axis=1)
                probs = jnp.exp2(products[keys] * (SCALING * LOG2E) + bias - log_total)
                ds_ref[keys, cols] = (probs * (dprobs[keys] - terms)).astype(bf16)
        dquery = tn(wink_ref[...], ds_ref[...]) * SCALING
        for h in range(QUERY_PER_KEY):
            dq_ref[a * BLOCK : (a + 1) * BLOCK, h * HEAD_SIZE : (h + 1) * HEAD_SIZE] = (
                dquery[:, h * BLOCK : (h + 1) * BLOCK].T.astype(bf16)
            )
        acc_ref[...] = nn(ds_ref[...], qs_ref[...])
        add_window(table_ref, place, acc_ref, sum_ref)
    o0[...] = sum_ref[0:512, :] * SCALING
    for i, out in enumerate((o1, o2, o3)):
        out[...] = (sum_ref[512 * (i + 1) : 512 * (i + 2), :] * SCALING).astype(bf16)


def project_kernel(
    table_ref, hidden, w0, w1, w2, w3, s0, s1, s2, s3,
    out, own_rows, r1, r2, r3, hidden_ref, all_ref, sems,
):
    copies = [
        pltpu.make_async_copy(
            hidden.at[:, i * QUARTER : (i + 1) * QUARTER],
            hidden_ref.at[:, i * QUARTER : (i + 1) * QUARTER],
            sems.at[i],
        )
        for i in range(4)
    ]
    for copy in copies:
        copy.start()
    for k, w in enumerate((w0, w1, w2, w3, s0, s1, s2, s3)):
        for i in range(4):
            at = pl.multiple_of(table_ref[k * 4 + i] * SLAB, BLOCK)
            all_ref[pl.ds(at, SLAB), :] = w[i * SLAB : (i + 1) * SLAB, :]
    own_rows[...] = all_ref[pl.ds(pl.multiple_of(table_ref[32] * QUARTER, BLOCK), QUARTER), :]
    for d, r in enumerate((r1, r2, r3)):
        r[...] = all_ref[pl.ds(pl.multiple_of(table_ref[33 + d] * HALF, BLOCK), HALF), :]
    total = jnp.zeros(out.shape, f32)
    for i, copy in enumerate(copies):
        copy.wait()
        part = slice(i * QUARTER, (i + 1) * QUARTER)
        total = total + nn(hidden_ref[:, part], all_ref[part, :])
    out[...] = total.astype(bf16)


def weight_kernel(table_ref, hidden, grads, r1, r2, r3, own, other, m1, m2, m3):
    turned = grads[...].T
    for k in range(16):
        for out, at in ((other, 16 + k), (own, k)):
            cols = pl.ds(pl.multiple_of(table_ref[at] * SLAB, BLOCK), SLAB)
            block = nn(turned, hidden[:, cols])
            out[k * HEAD_SIZE : (k + 1) * HEAD_SIZE, :] = block.astype(out.dtype)
    for r, m in ((r1, m1), (r2, m2), (r3, m3)):
        m[:HALF, :] = r[...]
        m[HALF:, :] = grads[...]


def input_kernel(table_ref, grads, own, a1, a2, a3, b1, b2, b3, out, rows_ref, grads_ref, sems):
    mine = pl.multiple_of(table_ref[36] * HALF, BLOCK)
    other = pl.multiple_of((1 - table_ref[36]) * HALF, BLOCK)
    copies = [pltpu.make_async_copy(own, rows_ref.at[:, 0:BLOCK], sems.at[0])]
    for d, (a, b) in enumerate(((a1, b1), (a2, b2), (a3, b3))):
        cols = slice((d + 1) * BLOCK, (d + 2) * BLOCK)
        pieces = (
            (a.at[0:HALF, :], rows_ref.at[pl.ds(mine, HALF), cols]),
            (b.at[0:HALF, :], rows_ref.at[pl.ds(other, HALF), cols]),
            (a.at[HALF : HALF + 256, :], grads_ref.at[:, cols]),
        )
        for i, (source, target) in enumerate(pieces):
            copies.append(pltpu.make_async_copy(source, target, sems.at[3 * d + 1 + i]))
    for copy in copies:
        copy.start()
    grads_ref[:, 0:BLOCK] = grads[...]
    for copy in copies:
        copy.wait()
    for part in range(4):
        cols = slice(part * 768, (part + 1) * 768)
        out[:, cols] = nt(grads_ref[...], rows_ref[cols, :]).astype(bf16)


SMEM = pl.BlockSpec(memory_space=pltpu.SMEM)
VMEM = pl.BlockSpec(memory_space=pltpu.VMEM)


def call(kernel, outs, ins, scratch=(), cost=1, smem=1, anys=(), limit=8):
    any_spec = pl.BlockSpec(memory_space=pl.ANY)
    specs = [SMEM] * smem + [any_spec if i in anys else VMEM for i in range(smem, len(ins))]
    return pl.pallas_call(
        kernel,
        out_shape=tuple(jax.ShapeDtypeStruct(s, d) for s, d in outs),
        in_specs=specs,
        out_specs=tuple(VMEM for _ in outs),
        scratch_shapes=[s if not isinstance(s, tuple) else pltpu.VMEM(*s) for s in scratch],
        compiler_params=pltpu.CompilerParams(vmem_limit_bytes=limit * 1024 * 1024),
        cost_estimate=pl.CostEstimate(
            flops=0, bytes_accessed=int(cost * COST_UNIT), transcendentals=0
        ),
    )(*ins)


def joined(parts):
    rows = sum(part.shape[0] for part in parts)
    (whole,) = call(
        join_kernel,
        [((rows, HEAD_SIZE), bf16)],
        parts,
        scratch=[pltpu.SemaphoreType.DMA],
        smem=0, anys=(0,),
    )
    return whole


def summed_along_z(own, *parts):
    for r, part in enumerate(parts):
        own = own + z_with(part, r + 1).astype(f32)
    return own


def local(
    hidden_in,
    queries,
    rotary_key_rows,
    value_projection,
    output_gradient,
    attended,
    doc_ids,
    block_place,
):
    dp = lax.axis_index("dp")
    ctx = lax.axis_index("ctx")
    x_hi, core = dp // 2, dp % 2
    x_lo, z = ctx // 4, ctx % 4
    x = x_hi * 2 + x_lo
    rows = queries.shape[1]
    grad_scale = float(rows * 32) ** (-0.5)
    query, grad, saved = queries[0], output_gradient[0], attended[0]

    def places_of_keys(placing):
        stored = jnp.arange(16, dtype=jnp.int32)
        owner = stored // 2
        lies = ((owner % 4) ^ z) * 4 + ((owner // 4) ^ x_lo) * 2 + stored % 2
        by_place = jnp.sum(jnp.where(placing[None, :] == stored[:, None], lies[None, :], 0), axis=1)
        mine = jnp.sum(
            jnp.where(stored[None, :] == (2 * ctx + jnp.arange(2))[:, None], placing[None, :], 0), axis=1
        )
        return jnp.concatenate([by_place, mine])

    def places_of_slabs(head):
        outer, inner = jnp.arange(16, dtype=jnp.int32) // 4, jnp.arange(16, dtype=jnp.int32) % 4

        def slabs_of(core):
            at_x = x ^ jnp.where(core == 0, outer, inner)
            at_z = z ^ jnp.where(core == 0, inner, outer)
            return (2 * (at_x // 2) + core) * 8 + (at_x % 2) * 4 + at_z

        asked = jnp.stack([head] + [2 * (head ^ d) + core for d in (1, 2, 3)] + [core])
        return jnp.concatenate([slabs_of(core), slabs_of(1 - core), asked]).astype(jnp.int32)

    hidden = hidden_in[0]
    window = ((SPAN, HEAD_SIZE), bf16)
    whole = ((2048, HEAD_SIZE), bf16)
    bias = ((SPAN, BLOCK), f32)
    square = ((SPAN, 1536), bf16)
    stack = ((1536, HEAD_SIZE), bf16)
    sums = [((SPAN, HEAD_SIZE), f32), ((2048, HEAD_SIZE), f32)]
    parts_out = [((512, HEAD_SIZE), f32)] + [((512, HEAD_SIZE), bf16)] * 3
    together = lax.optimization_barrier

    own_keys = rotary_key_rows[0]
    lowest = jnp.finfo(bf16).min
    near, first, placing, head, docs = together(
        (
            [jnp.maximum(own_keys, lowest), x_swap(own_keys)],
            [jnp.maximum(value_projection, lowest)] + [first_with(value_projection, r) for r in (1, 2, 3)],
            block_place[0],
            lax.axis_index("head"),
            jnp.maximum(doc_ids[0], 0).reshape(16, BLOCK),
        )
    )
    near, first = joined(near), joined(first)

    keys, w1, w3, first, table, slabs, first_query = together(
        (
            [near] + [z_with(near, r) for r in (1, 2, 3)],
            second_with(first, 1),
            second_with(first, 3),
            first,
            places_of_keys(placing),
            places_of_slabs(head),
            jnp.maximum(query, lowest),
        )
    )

    w2 = second_with(w3, 1)
    s0, s1, s3 = core_swap(first), core_swap(w1), core_swap(w3)
    totals, *value_parts = call(
        value_side_kernel,
        [((24, 128), f32)] + parts_out,
        [table, docs, first_query, grad, *keys],
        scratch=[((rows, 1536), bf16)] * 2
        + [whole, window, bias, ((SPAN, 256), f32), square, stack]
        + sums
        + [pltpu.SemaphoreType.DMA((2,))],
        anys=(2, 3), cost=7, limit=48,
    )
    w2, s0, s1, s3, totals, value_parts, slabs = together((w2, s0, s1, s3, totals, value_parts, slabs))

    s2 = core_swap(w2)
    own_values, own_rows, *halves = call(
        project_kernel,
        [((rows, HEAD_SIZE), bf16), ((QUARTER, HEAD_SIZE), bf16)] + [((HALF, HEAD_SIZE), bf16)] * 3,
        [slabs, hidden, first, w1, w2, w3, s0, s1, s2, s3],
        scratch=[
            ((rows, 4 * QUARTER), bf16),
            ((4 * QUARTER, HEAD_SIZE), bf16),
            pltpu.SemaphoreType.DMA((4,)),
        ],
        anys=(1,), cost=4, limit=48,
    )
    arrived = [z_with(part, r + 1) for r, part in enumerate(value_parts[1:])]
    own_values, halves = together((own_values, halves))

    near_values, value_sum = together(([own_values, x_swap(own_values)], value_parts[0]))
    near_values = joined(near_values)
    for part in arrived:
        value_sum = value_sum + part.astype(f32)
    value_rest = x_swap(value_sum.astype(bf16))[rows:]

    values = [near_values] + [z_with(near_values, r) for r in (1, 2, 3)]
    (terms,) = call(row_terms_kernel, [((24, 128), f32)], [grad, saved], smem=0)
    value_grads = (value_sum[:rows] + value_rest.astype(f32)).astype(bf16)

    message = ((HALF + rows, HEAD_SIZE), bf16)
    w_own, w_other, *messages = call(
        weight_kernel,
        [((2048, SLAB), f32), ((2048, SLAB), bf16)] + [message] * 3,
        [slabs, hidden, value_grads, *halves],
        cost=4, limit=24,
    )
    values, terms, w_own, w_other, messages, value_grads = together(
        (values, terms, w_own, w_other, messages, value_grads)
    )

    w_other = core_swap(w_other)
    w_parts = [
        w_own[512 * r : 512 * (r + 1)] + w_other[512 * r : 512 * (r + 1)].astype(f32) for r in range(4)
    ]
    w_parts = [w_parts[0]] + [part.astype(bf16) for part in w_parts[1:]]
    messages[0], messages[2] = y_with(messages[0], 1), y_with(messages[2], 3)
    w_got = [w_parts[0]] + [second_with(w_parts[r], r) for r in (1, 2, 3)]
    dquery, *key_parts = call(
        key_side_kernel,
        [((rows, 1536), bf16)] + parts_out,
        [table, docs, query, grad, totals, terms, *keys, *values],
        scratch=[whole, whole, window, window, bias, square, stack] + sums,
        cost=9, limit=28,
    )
    key_parts, w_got[:3], messages = together((key_parts, w_got[:3], messages))

    messages[1] = y_with(messages[1], 2)
    swapped = [core_swap(messages[0]), None, core_swap(messages[2])]
    key_parts[3], swapped = together((key_parts[3], swapped))
    arrived = [z_with(part, r + 1) for r, part in enumerate(key_parts[1:])]
    arrived[0], w_got = together((arrived[0], w_got))
    w_sum = w_got[0]
    for part in w_got[1:]:
        w_sum = w_sum + part.astype(f32)
    got = [
        first_with(w_sum[i * HEAD_SIZE : (i + 1) * HEAD_SIZE].astype(bf16), i) for i in (1, 2, 3)
    ]
    swapped[1] = core_swap(messages[1])
    arrived, key_sum, slabs, messages, swapped, got[:2] = together(
        (arrived, key_parts[0], slabs, messages, swapped, got[:2])
    )
    for part in arrived:
        key_sum = key_sum + part.astype(f32)

    key_rest = x_swap(key_sum[rows:].astype(bf16))
    (input_grad,) = call(
        input_kernel,
        [((rows, QUARTER), bf16)],
        [slabs, value_grads, own_rows, *messages, *swapped],
        scratch=[((QUARTER, 512), bf16), ((rows, 512), bf16), pltpu.SemaphoreType.DMA((10,))],
        anys=tuple(range(2, 9)),
        cost=4, limit=16,
    )
    got, input_grad, key_rest = together((got, input_grad, key_rest))
    key_grads = (key_sum[:rows] + key_rest.astype(f32)).astype(bf16)
    (weight_grad,) = call(
        functools.partial(fold_kernel, grad_scale),
        [((SLAB, HEAD_SIZE), f32)],
        [w_sum[:HEAD_SIZE], *got],
        smem=0,
    )
    return dquery[None], key_grads[None], input_grad[None], weight_grad


def solution(mesh):
    in_specs = (
        P("dp", "ctx", None),
        P("dp", "ctx", "head"),
        P("dp", "ctx", "head"),
        P(("dp", "ctx"), "head"),
        P("dp", "ctx", "head"),
        P("dp", "ctx", "head"),
        P("dp", None),
        P("dp", None),
    )
    out_specs = (
        P("dp", "ctx", "head"),
        P("dp", "ctx", "head"),
        P("dp", "ctx", "head"),
        P(("dp", "ctx"), "head"),
    )
    return jax.shard_map(local, mesh=mesh, in_specs=in_specs, out_specs=out_specs, check_vma=False)
```
